128 devices in a mesh: row: 8 (over x, core), col: 16 (over z, y).
Axes of the slice: x: 4, y: 4, z: 4, core: 2. Of those that a mesh axis runs over, the one named last changes fastest.
Arguments:
- atom_feats: bfloat16 [16384, 128], P(('row', 'col')), may hold values from -6 to 6
- atom_token: int32 [16384], P(('row', 'col')), may hold values from 0 to 2047, as said below
- atom_counts: int32 [2048], P('row'), may hold values from 1 to 15, as said below
- token_cond: bfloat16 [2048, 768], P('row'), may hold values from -6 to 6
- pair: bfloat16 [2048, 2048, 128], P('row', 'col'), may hold values from -5 to 5
- token_gain: float32 [768], replicated, may hold values from 0.25 to 1.75
- pair_gain: float32 [128], replicated, may hold values from 0.25 to 1.75
- w_bias: bfloat16 [128, 16], replicated, may hold values from -4 to 4
- w_agg: bfloat16 [128, 768], replicated, may hold values from -1.5 to 1.5
- w_query: bfloat16 [768, 768], replicated, may hold values from -0.3125 to 0.3125
- w_keyval: bfloat16 [768, 1536], replicated, may hold values from -0.3125 to 0.3125
- w_out: bfloat16 [768, 768], replicated, may hold values from -0.4375 to 0.4375
- w_back: bfloat16 [768, 128], replicated, may hold values from -0.21875 to 0.21875
Outputs:
- token_out: bfloat16 [2048, 768], P('row')
- atom_out: bfloat16 [16384, 128], P(('row', 'col'))
The draws below stay inside these ranges and needn't reach their ends.
Inputs may be any that keep to these rules, and one draw needn't show every extreme that they name: `atom_token`: atoms come in token order; the r-th block of 128 * 16 atoms belongs to tokens r * 256 to (r+1) * 256 - 1, every token has at least one atom. atom_counts[t] is the number of atoms with atom_token t; each block of 256 tokens has 2048 atoms.
All inputs are finite; a program needn't handle non-finite values.
Results may differ from the reference program's by a relative error of at most 0.023.
Values may be sent and summed in bfloat16 or wider, within the bound.
A program may use at most 128 MiB of HBM per device.

```python
import math
import jax
import jax.numpy as jnp
from jax import lax

CA = 128
D = 768
HEADS = 16
HD = 48
CZ = 128
TQ = 256
TOKENS = 2048
ATOMS = 16384
N_ROW = 8


def atom_layout(key):
    block_keys = jax.random.split(key, N_ROW)
    half = TQ // 2

    def one_block(block_key):
        first_key, second_key = jax.random.split(block_key)
        order = jax.random.permutation(first_key, TQ)
        moved = jax.random.randint(second_key, (half,), -7, 8)
        moved = moved.at[0].set(7)
        counts = jnp.full((TQ,), 8, jnp.int32)
        counts = counts.at[order[:half]].add(moved).at[order[half:2 * half]].add(-moved)
        ends = jnp.cumsum(counts)
        places = jnp.arange(8 * TQ, dtype=jnp.int32)
        owners = jnp.sum((ends[None, :] <= places[:, None]).astype(jnp.int32), axis=1)
        return (counts, owners)
    counts, owners = jax.vmap(one_block)(block_keys)
    offsets = (jnp.arange(N_ROW, dtype=jnp.int32) * TQ)[:, None]
    return (counts.reshape(-1).astype(jnp.int32), (owners + offsets).reshape(-1).astype(jnp.int32))


def bias_layout(key):
    key = jax.random.fold_in(key, 101)
    sign_key, head_key = jax.random.split(key)
    orders = jax.vmap(lambda single: jax.random.permutation(single, CZ))(jax.random.split(sign_key, HEADS))
    signs = jnp.where(orders < CZ // 2, 1.0, -1.0).astype(jnp.float32)
    head_order = jax.random.permutation(head_key, HEADS)
    strong_count = max(1, HEADS // 8)
    return (signs, head_order[:strong_count].astype(jnp.int32))


def draw_atom_counts(key, part):
    layout = atom_layout(key)
    return layout[0]


def draw_atom_token(key, part):
    layout = atom_layout(key)
    return layout[1]


def draw_w_bias(key, part):
    signs, strong_heads = bias_layout(key)
    key = jax.random.fold_in(key, 5)
    normal_key, level_key = jax.random.split(key)
    base = jnp.clip(jax.random.normal(normal_key, (CZ, HEADS), jnp.float32), -5.0, 5.0) * float(CZ // 4) ** (-0.5)
    level = jax.random.uniform(level_key, (CZ, HEADS), jnp.float32, 0.8, 1.2)
    strong = jnp.any(jnp.arange(HEADS, dtype=jnp.int32)[None, :] == strong_heads[:, None], axis=0)
    large_columns = 400.0 / CZ * jnp.transpose(signs) * level
    return jnp.where(strong[None, :], large_columns, base).astype(jnp.bfloat16)


def draw_pair(key, part):
    signs, strong_heads = bias_layout(key)
    key = jax.random.fold_in(key, 7)
    generic_key, noise_key, first_key, offset_key = jax.random.split(key, 4)
    full_shape = (TOKENS, TOKENS, CZ)
    generic = jnp.clip(jax.random.normal(generic_key, full_shape, jnp.float32), -4.0, 4.0)
    noise = jnp.clip(jax.random.normal(noise_key, (TOKENS, CZ), jnp.float32), -4.0, 4.0)
    positions = jnp.arange(TOKENS, dtype=jnp.int32)
    offset = jax.random.randint(offset_key, (), 0, 16)
    planted = positions % 16 == offset
    first = jax.random.randint(first_key, (TOKENS,), 0, TOKENS)
    second = (first + TOKENS // 2) % TOKENS
    strong_count = strong_heads.shape[0]
    row_head = strong_heads[positions // 16 % strong_count]
    strength = 0.5 * (positions // 16 % 3).astype(jnp.float32)
    pattern = signs[row_head] + strength[:, None] * noise
    chosen = (positions[None, :] == first[:, None]) | (positions[None, :] == second[:, None])
    hit = planted[:, None] & chosen
    return jnp.where(hit[:, :, None], pattern[:, None, :], generic).astype(jnp.bfloat16)


def level_of(key, shape, pieces, low, top_value):
    level, own = 1.0, jax.random.fold_in(key, 6)
    for position, shards_of in pieces:
        heights = jnp.exp(jax.random.uniform(jax.random.fold_in(own, position), (shards_of,), jnp.float32, low / len(pieces), top_value / len(pieces)))
        level = level * jnp.repeat(heights, shape[position] // shards_of).reshape([-1 if axis == position else 1 for axis in range(len(shape))])
    return level


def scatter_about(key, extent, scale, limit, pieces=(), kind=jnp.bfloat16):
    factor_of = level_of(key, extent, pieces, -0.22, 0.18) if pieces else 1.0
    drawn = jax.random.normal(key, extent, jnp.float32) * scale * factor_of
    return jnp.minimum(jnp.maximum(drawn, -limit), limit).astype(kind)


def setup_inputs(seed: int = 0) -> dict:
    arg_keys = jax.random.split(jax.random.key(seed), 14)
    return {
        "atom_feats": scatter_about(arg_keys[0], (ATOMS, CA), 1.0, 6.0, ((0, 128),)),
        "atom_token": draw_atom_token(jax.random.fold_in(arg_keys[13], 71), 0),
        "atom_counts": draw_atom_counts(jax.random.fold_in(arg_keys[13], 71), 0),
        "token_cond": scatter_about(arg_keys[3], (TOKENS, D), 1.0, 6.0, ((0, 8),)),
        "pair": draw_pair(jax.random.fold_in(arg_keys[13], 71), 0),
        "token_gain": jnp.clip(1.0 + 0.15 * jax.random.normal(arg_keys[5], (D,), jnp.float32), 0.25, 1.75),
        "pair_gain": jnp.clip(1.0 + 0.15 * jax.random.normal(arg_keys[6], (CZ,), jnp.float32), 0.25, 1.75),
        "w_bias": draw_w_bias(jax.random.fold_in(arg_keys[13], 71), 0),
        "w_agg": scatter_about(arg_keys[8], (CA, D), (CA // 8) ** -0.5, 1.5),
        "w_query": scatter_about(arg_keys[9], (D, D), (D // 2) ** -0.5, 0.3125),
        "w_keyval": scatter_about(arg_keys[10], (D, 2 * D), (D // 2) ** -0.5, 0.3125),
        "w_out": scatter_about(arg_keys[11], (D, D), (D // 4) ** -0.5, 0.4375),
        "w_back": scatter_about(arg_keys[12], (D, CA), D ** -0.5, 0.21875),
    }


def normalize(values):
    center = values - lax.optimization_barrier(jnp.mean(values, axis=-1, keepdims=True))
    spread = lax.optimization_barrier(jnp.mean(center * center, axis=-1, keepdims=True))
    return center * lax.rsqrt(spread + 1e-05)

def reference(atom_feats, atom_token, atom_counts, token_cond, pair, token_gain, pair_gain, w_bias, w_agg, w_query, w_keyval, w_out, w_back):
    sums = jax.ops.segment_sum(atom_feats.astype(jnp.float32), atom_token, num_segments=TOKENS)
    mean_feats = sums / atom_counts.astype(jnp.float32)[:, None]
    agg = jnp.dot(mean_feats, w_agg.astype(jnp.float32), precision=lax.Precision.HIGHEST)
    hidden = agg + token_cond.astype(jnp.float32)
    normed = (normalize(hidden) * token_gain).astype(jnp.bfloat16)
    query = (jnp.dot(normed, w_query, preferred_element_type=jnp.float32) / math.sqrt(HD)).astype(jnp.bfloat16)
    keyval = jnp.dot(normed, w_keyval, preferred_element_type=jnp.float32).astype(jnp.bfloat16)
    query = lax.optimization_barrier(query)
    keyval = lax.optimization_barrier(keyval)
    keys = keyval[:, :D].reshape(TOKENS, HEADS, HD).astype(jnp.float32)
    values = keyval[:, D:].reshape(TOKENS, HEADS, HD).astype(jnp.float32)
    gain_weight = (pair_gain[:, None] * w_bias.astype(jnp.float32)).astype(jnp.bfloat16)
    gain_weight = lax.optimization_barrier(gain_weight).astype(jnp.float32)
    block = math.gcd(TOKENS, 64)

    def attend(index):
        start = (index * block).astype(jnp.int32)
        q_block = lax.dynamic_slice_in_dim(query, start, block, 0).reshape(block, HEADS, HD).astype(jnp.float32)
        p_block = lax.dynamic_slice_in_dim(pair, start, block, 0).astype(jnp.float32)
        bias = jnp.einsum('ijc,ch->hij', normalize(p_block), gain_weight, precision=lax.Precision.HIGHEST)
        scores = jnp.einsum('ihd,jhd->hij', q_block, keys, precision=lax.Precision.HIGHEST) + bias
        top = lax.optimization_barrier(jnp.max(scores, axis=-1, keepdims=True))
        expo = jnp.exp(scores - top)
        total = lax.optimization_barrier(jnp.sum(expo, axis=-1))
        probs = lax.optimization_barrier(expo.astype(jnp.bfloat16)).astype(jnp.float32)
        weighted = jnp.einsum('hij,jhd->ihd', probs, values, precision=lax.Precision.HIGHEST)
        return (weighted / jnp.transpose(total)[:, :, None]).reshape(block, D)
    attn = lax.map(attend, jnp.arange(TOKENS // block, dtype=jnp.int32)).reshape(TOKENS, D).astype(jnp.bfloat16)
    token_out = (hidden + jnp.dot(attn, w_out, preferred_element_type=jnp.float32)).astype(jnp.bfloat16)
    back = jnp.dot(token_out, w_back, preferred_element_type=jnp.float32)
    picked = jnp.take(back, atom_token, axis=0)
    atom_out = (atom_feats.astype(jnp.float32) + picked).astype(jnp.bfloat16)
    return (token_out, atom_out)
```

```python
import math

import jax
import jax.numpy as jnp
from jax import lax
from jax.experimental import pallas as pl
from jax.experimental.pallas import tpu as pltpu
from jax.sharding import PartitionSpec as P

D = 768
HEADS = 16
HD = 48
CA = 128
TQ = 256
TK = 128
NCOL = 16
NROW = 8
OWN = TQ // NCOL
MSG = D + 128
CHUNK = 128
PAIR_PARTS = 8
PART_ROWS = TQ // PAIR_PARTS
FIRST_PARTS = 3
PASS_PART = 6
MESH = pl.DeviceIdType.MESH
F32 = jnp.float32
BF16 = jnp.bfloat16


def mm(a, b):
    return jnp.dot(a, b, preferred_element_type=F32)


def mm_nt(a, b):
    return lax.dot_general(a, b, (((1,), (1,)), ((), ())), preferred_element_type=F32)


def iota(shape, axis):
    return lax.broadcasted_iota(jnp.int32, shape, axis)


def split(x):
    high = x.astype(BF16)
    low = (x - high.astype(F32)).astype(BF16)
    return high, low


def rows_of(index, size):
    return pl.ds(pl.multiple_of(index * size, size), size)


def kernel(
    feats_h, tok_h, counts_h, cond_h, pair_h, tgain_h, pgain_h, wbias_h, wagg_h, wq_h, wkv_h, wo_h, wb_h,
    token_out_h, atom_out_h,
    feats, tok, counts, cond, pair, tgain, pgain, wbias, wagg, wq, wkv, wo, wb,
    gmat, colsum, bias, s1, s2, part, abuf, means, mean_own, cnt, aggv, normed, qv, kv, keymeans, keycond,
    km, vm, probs, wmsg, cbuf, expand, tokbuf, pick, atomv,
    lsem, psem, osem, asem, bsem, ksem, csem, qsem, dsem,
):
    r = lax.axis_index("row")
    c = lax.axis_index("col")
    key_col = 2 * r + lax.shift_right_logical(c, 3)
    key_slot = jnp.bitwise_and(c, 7)
    src_row = lax.shift_right_logical(c, 1)
    src_col = 8 * jnp.bitwise_and(c, 1)
    is_self = c == key_col
    other = jnp.logical_not(is_self)
    holds = r == src_row
    same_core = jnp.bitwise_and(r, 1) == jnp.bitwise_and(src_row, 1)
    sibling = jnp.bitwise_xor(r, 1)
    passes_on = jnp.logical_and(same_core, jnp.logical_not(holds))

    def col_at(offset):
        return jnp.bitwise_and(c + offset, NCOL - 1)

    next_col = col_at(1)

    def local(i, src, dst):
        return pltpu.make_async_copy(src, dst, lsem.at[i])

    loads = {
        "feats": local(0, feats_h, feats),
        "tok": local(1, tok_h, tok),
        "counts": local(2, counts_h, counts),
        "wbias": local(3, wbias_h, wbias),
        "pgain": local(4, pgain_h, pgain),
        "wagg": local(5, wagg_h, wagg),
        "cond": local(7, cond_h, cond),
        "tgain": local(8, tgain_h, tgain),
        "wq": local(9, wq_h, wq),
        "wkv": local(10, wkv_h, wkv),
        "wo": local(11, wo_h, wo),
        "wb": local(12, wb_h, wb),
    }

    def pair_load(k):
        at = pl.ds(k * PART_ROWS, PART_ROWS)
        return pltpu.make_async_copy(pair_h.at[at], pair.at[at], psem.at[k])

    for name in ("feats", "tok", "counts", "wbias", "pgain"):
        loads[name].start()

    barrier = pltpu.get_barrier_semaphore()

    def greet(row, col):
        pl.semaphore_signal(barrier, inc=1, device_id=(row, col), device_id_type=MESH)

    for k in range(1, NCOL):
        greet(r, col_at(k))
    for k in range(1, 8):
        greet(src_row, src_col + jnp.bitwise_and(c + k, 7))

    @pl.when(other)
    def _():
        greet(src_row, src_col + key_slot)

    @pl.when(jnp.logical_not(holds))
    def _():
        greet(jnp.where(same_core, src_row, sibling), c)

    for k in range(FIRST_PARTS):
        pair_load(k).start()

    loads["feats"].wait()
    loads["tok"].wait()
    here = tok[...] - r * TQ
    member = jnp.where(iota((TQ, CA), 0) == here, 1.0, 0.0).astype(BF16)
    part[...] = mm(member, feats[...]).astype(BF16)

    pl.semaphore_wait(
        barrier,
        NCOL - 1 + 8 - is_self.astype(jnp.int32) + 4 * holds.astype(jnp.int32) + passes_on.astype(jnp.int32))

    def remote(src, dst, sems, row, col):
        return pltpu.make_async_remote_copy(
            src_ref=src, dst_ref=dst, send_sem=sems.at[0], recv_sem=sems.at[1],
            device_id=(row, col), device_id_type=MESH)

    others = pl.ds(0, NCOL - 1)
    other_rows = pl.ds(0, (NCOL - 1) * OWN)

    def a_copy(peer):
        return remote(part.at[rows_of(peer, OWN)], abuf.at[c], asem, r, peer)

    a_all = remote(part.at[other_rows], abuf.at[others], asem, r, next_col)

    def each_peer(action):
        for k in (8, 9, 10, 11, 12, 13, 14, 15, 1, 2, 3, 4, 5, 6, 7):
            action(col_at(k))

    each_peer(lambda peer: a_copy(peer).start())
    for name in ("wagg", "cond", "tgain"):
        loads[name].start()
    for k in range(FIRST_PARTS, PAIR_PARTS):
        pair_load(k).start()
    for name in ("wq", "wkv", "wo", "wb"):
        loads[name].start()

    def each_target(action):
        for k in range(1, NROW):
            action(jnp.bitwise_and(r + k, NROW - 1))

        @pl.when(other)
        def _():
            action(r)

    def from_sources(buffer, sems, action):
        for count in (7, 8):
            @pl.when(is_self == (count == 7))
            def _():
                action(remote(buffer.at[pl.ds(0, count)], buffer.at[pl.ds(0, count)], sems, r, next_col))

    held_cond = cond_h.at[rows_of(jnp.bitwise_and(c, 1), TK)]

    def cond_copy(source, row):
        return remote(source, keycond, qsem, row, c)

    @pl.when(holds)
    def _():
        for k in (4, 2, 6):
            cond_copy(held_cond, jnp.bitwise_and(r + k, NROW - 1)).start()
        cond_copy(held_cond, sibling).start()

    abuf[c] = part[rows_of(c, OWN), :]

    eye = iota((CA, CA), 0) == iota((CA, CA), 1)
    eye_b = jnp.where(eye, 1.0, 0.0).astype(BF16)
    pick[...] = mm_nt(eye_b, member).astype(BF16)
    loads["wbias"].wait()
    loads["pgain"].wait()
    gain_t = (wbias[...].astype(F32) * pgain[...]).astype(BF16)
    none = jnp.zeros((HEADS, CA), BF16)
    place = iota((HEADS, CA), 0)
    ones_left = jnp.where(place == 0, 1.0, 0.0).astype(BF16)
    ones_right = jnp.where(place == 1, 1.0, 0.0).astype(BF16)
    gmat[:, 0:CA] = jnp.concatenate([gain_t, none, ones_left], axis=0)
    gmat[:, CA:2 * CA] = jnp.concatenate([none, gain_t, ones_right], axis=0)
    colsum[...] = jnp.broadcast_to(jnp.sum(gain_t.astype(F32), axis=1, keepdims=True), (HEADS, CA))
    loads["counts"].wait()
    for half in range(2):
        line = counts[:, half * CA:(half + 1) * CA].astype(F32)
        column = jnp.sum(jnp.where(eye, jnp.broadcast_to(line, (CA, CA)), 0.0), axis=1, keepdims=True)
        cnt[half * CA:(half + 1) * CA, :] = jnp.broadcast_to(column, (CA, CA))

    def bias_rows(k):
        pair_load(k).wait()

        def four(j, carry):
            first = k * PART_ROWS + 4 * j
            blocks = [jnp.transpose(pair[first + e]) for e in range(4)]
            for e in range(4):
                wide = blocks[e].astype(F32)
                s2[pl.ds(first + e, 1), :] = jnp.sum(wide * wide, axis=0, keepdims=True)
            square = jnp.concatenate(
                [jnp.concatenate(blocks[0:2], axis=1), jnp.concatenate(blocks[2:4], axis=1)], axis=0)
            sums = mm(gmat[...], square)
            for e in range(4):
                low, side = e // 2, slice((e % 2) * CA, (e % 2 + 1) * CA)
                bias[pl.ds(first + e, HEADS, stride=TQ), :] = sums[low * HEADS:(low + 1) * HEADS, side]
                s1[pl.ds(first + e, 1), :] = sums[2 * HEADS + low:2 * HEADS + low + 1, side]
            return carry

        lax.fori_loop(0, PART_ROWS // 4, four, 0, unroll=4)

    for k in range(FIRST_PARTS):
        bias_rows(k)

    a_all.wait_recv()
    own = rows_of(c, OWN)
    mean_own[...] = jnp.sum(abuf[...].astype(F32), axis=0) / cnt[own, :]
    means[own, :] = mean_own[...].astype(BF16)

    def k_copy(target):
        return remote(means.at[own], keymeans.at[key_slot], ksem, target, key_col)

    def b_copy(peer):
        return remote(means.at[own], means.at[own], bsem, r, peer)

    b_all = remote(means.at[other_rows], means.at[other_rows], bsem, r, next_col)
    each_target(lambda target: k_copy(target).start())
    each_peer(lambda peer: b_copy(peer).start())

    @pl.when(is_self)
    def _():
        keymeans[key_slot] = means[own, :]

    for k in range(FIRST_PARTS, PASS_PART):
        bias_rows(k)

    @pl.when(passes_on)
    def _():
        arrived = cond_copy(keycond, sibling)
        arrived.wait_recv()
        arrived.start()

    for k in range(PASS_PART, PAIR_PARTS):
        bias_rows(k)

    def normalize(hidden):
        center = hidden - jnp.mean(hidden, axis=-1, keepdims=True)
        spread = jnp.mean(center * center, axis=-1, keepdims=True)
        gain = jnp.concatenate([tgain[k:k + 1, :] for k in range(6)], axis=1)
        return (center * lax.rsqrt(spread + 1e-05) * gain).astype(BF16)

    for name in ("wagg", "cond", "tgain", "wq", "wkv"):
        loads[name].wait()
    @pl.when(holds)
    def _():
        keycond[...] = cond[rows_of(jnp.bitwise_and(c, 1), TK), :]

    @pl.when(jnp.logical_not(same_core))
    def _():
        cond_copy(keycond, sibling).wait_recv()

    from_sources(keymeans, ksem, lambda copy: copy.wait_recv())
    b_all.wait_recv()
    key_agg = mm(keymeans[...].reshape(TK, CA), wagg[...])
    aggv[...] = mm(means[...], wagg[...])
    key_rows = normalize(key_agg + keycond[...].astype(F32))
    for n in range(6):
        cols = slice(n * 256, (n + 1) * 256)
        kv[:, cols] = mm(key_rows, wkv[:, cols]).astype(BF16)
    for k in range(TQ // 64):
        at = slice(k * 64, (k + 1) * 64)
        normed[at, :] = normalize(aggv[at, :] + cond[at, :].astype(F32))
    for n in range(3):
        cols = slice(n * 256, (n + 1) * 256)
        qv[:, cols] = (mm(normed[...], wq[:, cols]) * (1.0 / math.sqrt(HD))).astype(BF16)

    def head_mask(first, width, head):
        lane = iota((1, width), 1) + first
        return jnp.where(jnp.logical_and(lane >= head * HD, lane < (head + 1) * HD), 1.0, 0.0).astype(BF16)

    windows = []
    for p in range(HEADS // 2):
        first = (2 * p * HD) // 128 * 128
        last = -(-((2 * p + 2) * HD) // 128) * 128
        windows.append((first, last - first))
        block = kv[:, first:last]
        for e in range(2):
            km[p, e * TK:(e + 1) * TK, 0:last - first] = block * head_mask(first, last - first, 2 * p + e)
    value_heads = []
    for n in range(3):
        heads = [h for h in range(HEADS) if h * HD < (n + 1) * 256 and (h + 1) * HD > n * 256]
        value_heads.append(heads)
        block = kv[:, D + n * 256:D + (n + 1) * 256]
        for slot, h in enumerate(heads):
            vm[n, slot * TK:(slot + 1) * TK, :] = block * head_mask(n * 256, 256, h)

    def c_copy(owner):
        return remote(wmsg.at[rows_of(owner, OWN)], cbuf.at[c], csem, r, owner)

    c_all = remote(wmsg.at[other_rows], cbuf.at[others], csem, r, next_col)
    owners = CHUNK // OWN
    chunks = TQ // CHUNK

    def attend(step):
        chunk = jnp.bitwise_and(lax.shift_right_logical(c, 3) + step, chunks - 1)
        at = rows_of(chunk, CHUNK)
        mean = s1[at, :] * (1.0 / CA)
        mean_high, mean_low = split(mean)
        mean_high = mean_high.astype(F32)
        mean_low = mean - mean_high
        var = (s2[at, :] * (1.0 / CA) - mean_high * mean_high) - mean_low * (mean_high + mean)
        rstd = lax.rsqrt(jnp.maximum(var, 0.0) + 1e-05)
        lane = iota((CHUNK, 128), 1)
        tops = jnp.zeros((CHUNK, 128), F32)
        totals = jnp.zeros((CHUNK, 128), F32)
        for p in range(HEADS // 2):
            first, width = windows[p]
            scores = mm_nt(qv[at, first:first + width], km[p, :, 0:width])
            for e in range(2):
                h = 2 * p + e
                raw = bias[pl.ds(pl.multiple_of(h * TQ + chunk * CHUNK, CHUNK), CHUNK), :]
                sc = scores[:, e * TK:(e + 1) * TK] + (raw - mean * colsum[h:h + 1, :]) * rstd
                top = jnp.max(sc, axis=-1, keepdims=True)
                expo = jnp.exp(sc - top)
                total = jnp.sum(expo, axis=-1, keepdims=True)
                probs[:, h * TK:(h + 1) * TK] = expo.astype(BF16)
                tops = jnp.where(lane == h, top, tops)
                totals = jnp.where(lane == h, total, totals)
        for n in range(3):
            heads = value_heads[n]
            wide = probs[:, heads[0] * TK:(heads[-1] + 1) * TK]
            wmsg[at, n * 256:(n + 1) * 256] = mm(wide, vm[n]).astype(BF16)
        tops_high, tops_mid = split(tops)
        tops_low = (tops - tops_high.astype(F32) - tops_mid.astype(F32)).astype(BF16)
        totals_high, totals_low = split(totals)
        stats = tops_high.astype(F32)
        for place, piece in enumerate((tops_mid, tops_low, totals_high, totals_low)):
            stats = stats + pltpu.roll(piece.astype(F32), (place + 1) * HEADS, 1)
        wmsg[at, D:MSG] = stats.astype(BF16)

        return chunk

    def far_chunk(step, carry):
        chunk = attend(step)
        for k in range(owners):
            c_copy(chunk * owners + jnp.bitwise_and(c + k, owners - 1)).start()
        return carry

    lax.fori_loop(1, chunks, far_chunk, 0)
    chunk = attend(0)
    for k in range(1, owners):
        c_copy(chunk * owners + jnp.bitwise_and(c + k, owners - 1)).start()
    cbuf[c] = wmsg[own, :]
    mean_high, mean_low = split(mean_own[...])
    hidden_own = mm(mean_high, wagg[...]) + mm(mean_low, wagg[...]) + cond[own, :].astype(F32)
    spread_row = jnp.bitwise_and(iota((256, D), 0), 127)
    spread_col = iota((256, D), 1) - spread_row * HD
    expand[...] = jnp.where(jnp.logical_and(spread_col >= 0, spread_col < HD), 1.0, 0.0).astype(BF16)
    loads["wo"].wait()
    loads["wb"].wait()
    c_all.wait_recv()

    stat = cbuf[:, :, D:MSG].reshape(TQ, 128).astype(F32)
    def piece(k):
        return pltpu.roll(stat, 128 - k * HEADS, 1)

    tops = ((stat + piece(1)) + piece(2)).reshape(NCOL, OWN, 128)
    totals = (piece(3) + piece(4)).reshape(NCOL, OWN, 128)
    best = jnp.max(tops, axis=0, keepdims=True)
    scale = jnp.exp(tops - best)
    total = jnp.sum(scale * totals, axis=0, keepdims=True)
    valid = iota((1, 1, 128), 2) < HEADS
    total = jnp.where(valid, total, 1.0)
    factor = jnp.where(valid, scale / total, 0.0).reshape(TQ, 128)
    factor = jnp.concatenate(split(factor), axis=1)
    attn_parts = []
    for n in range(3):
        cols = slice(n * 256, (n + 1) * 256)
        wide = mm(factor, expand[:, cols])
        terms = cbuf[:, :, cols].astype(F32) * wide.reshape(NCOL, OWN, 256)
        attn_parts.append(jnp.sum(terms, axis=0).astype(BF16))
    attn = jnp.concatenate(attn_parts, axis=1)
    finished = (hidden_own + mm(attn, wo[...])).astype(BF16)

    tokbuf[c] = finished
    d_all = remote(tokbuf.at[others], tokbuf.at[others], dsem, r, next_col)
    each_peer(lambda peer: remote(tokbuf.at[c], tokbuf.at[c], dsem, r, peer).start())

    a_all.wait_send()
    b_all.wait_send()

    @pl.when(holds)
    def _():
        for k in range(4):
            cond_copy(held_cond, sibling).wait_send()

    @pl.when(passes_on)
    def _():
        cond_copy(keycond, sibling).wait_send()

    from_sources(keymeans, ksem, lambda copy: copy.wait_send())
    c_all.wait_send()

    d_all.wait_recv()
    token_store = pltpu.make_async_copy(tokbuf, token_out_h, osem.at[0])
    token_store.start()
    chosen = mm(pick[...], tokbuf[...].reshape(TQ, D)).astype(BF16)
    atomv[...] = (feats[...].astype(F32) + mm(chosen, wb[...])).astype(BF16)
    atom_store = pltpu.make_async_copy(atomv, atom_out_h, osem.at[1])
    atom_store.start()
    d_all.wait_send()
    token_store.wait()
    atom_store.wait()


def hand_over(token_in, atom_in, token_out, atom_out, sems):
    copies = [
        pltpu.make_async_copy(token_in, token_out, sems.at[0]),
        pltpu.make_async_copy(atom_in, atom_out, sems.at[1]),
    ]
    for copy in copies:
        copy.start()
    for copy in copies:
        copy.wait()


def local(
    atom_feats, atom_token, atom_counts, token_cond, pair, token_gain, pair_gain, w_bias, w_agg, w_query, w_keyval,
    w_out, w_back,
):
    any_space = pl.BlockSpec(memory_space=pl.ANY)
    hbm = pl.BlockSpec(memory_space=pltpu.HBM)
    vmem = pltpu.VMEM
    dma = pltpu.SemaphoreType.DMA
    scratch = [
        vmem((CA, CA), BF16), vmem((1, CA), jnp.int32), vmem((1, TQ), jnp.int32), vmem((TQ, D), BF16),
        vmem((TQ, TK, CA), BF16), vmem((6, 128), F32), vmem((1, CA), F32), vmem((HEADS, CA), BF16),
        vmem((CA, D), BF16), vmem((D, D), BF16), vmem((D, 2 * D), BF16), vmem((D, D), BF16), vmem((D, CA), BF16),
        vmem((3 * HEADS, 2 * CA), BF16), vmem((HEADS, CA), F32), vmem((HEADS * TQ, TK), F32), vmem((TQ, TK), F32),
        vmem((TQ, TK), F32), vmem((TQ, CA), BF16), vmem((NCOL, OWN, CA), BF16), vmem((TQ, CA), BF16), vmem((OWN, CA), F32),
        vmem((TQ, CA), F32),
        vmem((TQ, D), F32), vmem((TQ, D), BF16), vmem((TQ, D), BF16), vmem((TK, 2 * D), BF16),
        vmem((8, OWN, CA), BF16), vmem((TK, D), BF16),
        vmem((HEADS // 2, 2 * TK, 256), BF16), vmem((3, 6 * TK, 256), BF16), vmem((CHUNK, HEADS * TK), BF16),
        vmem((TQ, MSG), BF16), vmem((NCOL, OWN, MSG), BF16), vmem((256, D), BF16), vmem((NCOL, OWN, D), BF16),
        vmem((CA, TQ), BF16), vmem((CA, CA), BF16),
        dma((13,)), dma((PAIR_PARTS,)), dma((2,)),
        *[dma((2,))] * 6,
    ]
    outs = pl.pallas_call(
        kernel,
        out_shape=(jax.ShapeDtypeStruct((NCOL, OWN, D), BF16), jax.ShapeDtypeStruct((CA, CA), BF16)),
        in_specs=[hbm] * 13,
        out_specs=(any_space, any_space),
        scratch_shapes=scratch,
        compiler_params=pltpu.CompilerParams(
            collective_id=0, has_side_effects=True, vmem_limit_bytes=40 * 1024 * 1024),
        name="diffusion_block",
    )(*[pltpu.with_memory_space_constraint(x, pltpu.HBM) for x in (
        atom_feats, atom_token.reshape(1, CA), atom_counts.reshape(1, TQ), token_cond, pair, token_gain.reshape(6, 128),
        pair_gain.reshape(1, CA), w_bias.T, w_agg, w_query, w_keyval, w_out, w_back,
    )])
    stored = pl.pallas_call(
        hand_over,
        out_shape=(jax.ShapeDtypeStruct((NCOL, OWN, D), BF16), jax.ShapeDtypeStruct((CA, CA), BF16)),
        in_specs=[any_space] * 2,
        out_specs=(any_space, any_space),
        scratch_shapes=[dma((2,))],
        compiler_params=pltpu.CompilerParams(vmem_limit_bytes=1024 * 1024),
        name="hand_over",
    )(*outs)
    return stored[0].reshape(TQ, D), stored[1]


def solution(mesh):
    placed = (
        P(("row", "col"), None), P(("row", "col")), P("row"), P("row", None), P("row", "col", None),
        P(), P(), P(), P(), P(), P(), P(), P(),
    )
    return jax.shard_map(
        local,
        mesh=mesh,
        in_specs=placed,
        out_specs=(P("row", None), P(("row", "col"), None)),
        check_vma=False,
    )
```

```python
import math

import jax
import jax.numpy as jnp
from jax import lax
from jax.experimental import pallas as pl
from jax.experimental.pallas import tpu as pltpu
from jax.sharding import PartitionSpec as P

D = 768
HEADS = 16
HD = 48
CA = 128
TQ = 256
TK = 128
NCOL = 16
NROW = 8
OWN = TQ // NCOL
MSG = D + 128
CHUNK = 128
PAIR_PARTS = 8
PART_ROWS = TQ // PAIR_PARTS
FIRST_PARTS = 3
PASS_PART = 6
MESH = pl.DeviceIdType.MESH
F32 = jnp.float32
BF16 = jnp.bfloat16


def mm(a, b):
    return jnp.dot(a, b, preferred_element_type=F32)


def mm_nt(a, b):
    return lax.dot_general(a, b, (((1,), (1,)), ((), ())), preferred_element_type=F32)


def iota(shape, axis):
    return lax.broadcasted_iota(jnp.int32, shape, axis)


def split(x):
    high = x.astype(BF16)
    low = (x - high.astype(F32)).astype(BF16)
    return high, low


def rows_of(index, size):
    return pl.ds(pl.multiple_of(index * size, size), size)


def kernel(
    feats_h, tok_h, counts_h, cond_h, pair_h, tgain_h, pgain_h, wbias_h, wagg_h, wq_h, wkv_h, wo_h, wb_h,
    token_out_h, atom_out_h,
    feats, tok, counts, cond, pair, tgain, pgain, wbias, wagg, wq, wkv, wo, wb,
    gmat, colsum, bias, s1, s2, part, abuf, means, mean_own, cnt, aggv, normed, qv, kv, keymeans, keycond,
    km, vm, probs, wmsg, cbuf, expand, tokbuf, pick, atomv, head_ones,
    lsem, psem, osem, asem, bsem, ksem, csem, qsem, dsem,
):
    r = lax.axis_index("row")
    c = lax.axis_index("col")
    key_col = 2 * r + lax.shift_right_logical(c, 3)
    key_slot = jnp.bitwise_and(c, 7)
    src_row = lax.shift_right_logical(c, 1)
    src_col = 8 * jnp.bitwise_and(c, 1)
    is_self = c == key_col
    other = jnp.logical_not(is_self)
    holds = r == src_row
    same_core = jnp.bitwise_and(r, 1) == jnp.bitwise_and(src_row, 1)
    sibling = jnp.bitwise_xor(r, 1)
    passes_on = jnp.logical_and(same_core, jnp.logical_not(holds))

    def col_at(offset):
        return jnp.bitwise_and(c + offset, NCOL - 1)

    next_col = col_at(1)

    def local(i, src, dst):
        return pltpu.make_async_copy(src, dst, lsem.at[i])

    loads = {
        "feats": local(0, feats_h, feats),
        "tok": local(1, tok_h, tok),
        "counts": local(2, counts_h, counts),
        "wbias": local(3, wbias_h, wbias),
        "pgain": local(4, pgain_h, pgain),
        "wagg": local(5, wagg_h, wagg),
        "cond": local(7, cond_h, cond),
        "tgain": local(8, tgain_h, tgain),
        "wq": local(9, wq_h, wq),
        "wkv": local(10, wkv_h, wkv),
        "wo": local(11, wo_h, wo),
        "wb": local(12, wb_h, wb),
    }

    def pair_load(k):
        at = pl.ds(k * PART_ROWS, PART_ROWS)
        return pltpu.make_async_copy(pair_h.at[at], pair.at[at], psem.at[k])

    for name in ("feats", "tok", "counts", "wbias", "pgain"):
        loads[name].start()

    barrier = pltpu.get_barrier_semaphore()

    def greet(row, col):
        pl.semaphore_signal(barrier, inc=1, device_id=(row, col), device_id_type=MESH)

    for k in range(1, NCOL):
        greet(r, col_at(k))
    for k in range(1, 8):
        greet(src_row, src_col + jnp.bitwise_and(c + k, 7))

    @pl.when(other)
    def _():
        greet(src_row, src_col + key_slot)

    @pl.when(jnp.logical_not(holds))
    def _():
        greet(jnp.where(same_core, src_row, sibling), c)

    for k in range(FIRST_PARTS):
        pair_load(k).start()

    loads["feats"].wait()
    loads["tok"].wait()
    here = tok[...] - r * TQ
    member = jnp.where(iota((TQ, CA), 0) == here, 1.0, 0.0).astype(BF16)
    part[...] = mm(member, feats[...]).astype(BF16)

    pl.semaphore_wait(
        barrier,
        NCOL - 1 + 8 - is_self.astype(jnp.int32) + 4 * holds.astype(jnp.int32) + passes_on.astype(jnp.int32))

    def remote(src, dst, sems, row, col):
        return pltpu.make_async_remote_copy(
            src_ref=src, dst_ref=dst, send_sem=sems.at[0], recv_sem=sems.at[1],
            device_id=(row, col), device_id_type=MESH)

    others = pl.ds(0, NCOL - 1)
    other_rows = pl.ds(0, (NCOL - 1) * OWN)

    def a_copy(peer):
        return remote(part.at[rows_of(peer, OWN)], abuf.at[c], asem, r, peer)

    a_all = remote(part.at[other_rows], abuf.at[others], asem, r, next_col)

    def each_peer(action):
        for k in (8, 9, 10, 11, 12, 13, 14, 15, 1, 2, 3, 4, 5, 6, 7):
            action(col_at(k))

    each_peer(lambda peer: a_copy(peer).start())
    for name in ("wagg", "cond", "tgain"):
        loads[name].start()
    for k in range(FIRST_PARTS, PAIR_PARTS):
        pair_load(k).start()
    for name in ("wq", "wkv", "wo", "wb"):
        loads[name].start()

    def each_target(action):
        for k in range(1, NROW):
            action(jnp.bitwise_and(r + k, NROW - 1))

        @pl.when(other)
        def _():
            action(r)

    def from_sources(buffer, sems, action):
        for count in (7, 8):
            @pl.when(is_self == (count == 7))
            def _():
                action(remote(buffer.at[pl.ds(0, count)], buffer.at[pl.ds(0, count)], sems, r, next_col))

    held_cond = cond_h.at[rows_of(jnp.bitwise_and(c, 1), TK)]

    def cond_copy(source, row):
        return remote(source, keycond, qsem, row, c)

    @pl.when(holds)
    def _():
        for k in (4, 2, 6):
            cond_copy(held_cond, jnp.bitwise_and(r + k, NROW - 1)).start()
        cond_copy(held_cond, sibling).start()

    abuf[c] = part[rows_of(c, OWN), :]

    for h in range(HEADS):
        head_ones[h * TK:(h + 1) * TK, :] = jnp.where(iota((TK, 128), 1) == h, 1.0, 0.0).astype(BF16)
    eye = iota((CA, CA), 0) == iota((CA, CA), 1)
    eye_b = jnp.where(eye, 1.0, 0.0).astype(BF16)
    pick[...] = mm_nt(eye_b, member).astype(BF16)
    loads["wbias"].wait()
    loads["pgain"].wait()
    gain_t = (wbias[...].astype(F32) * pgain[...]).astype(BF16)
    none = jnp.zeros((HEADS, CA), BF16)
    place = iota((HEADS, CA), 0)
    ones_left = jnp.where(place == 0, 1.0, 0.0).astype(BF16)
    ones_right = jnp.where(place == 1, 1.0, 0.0).astype(BF16)
    gmat[:, 0:CA] = jnp.concatenate([gain_t, none, ones_left], axis=0)
    gmat[:, CA:2 * CA] = jnp.concatenate([none, gain_t, ones_right], axis=0)
    colsum[...] = jnp.broadcast_to(jnp.sum(gain_t.astype(F32), axis=1, keepdims=True), (HEADS, CA))
    loads["counts"].wait()
    for half in range(2):
        line = counts[:, half * CA:(half + 1) * CA].astype(F32)
        column = jnp.sum(jnp.where(eye, jnp.broadcast_to(line, (CA, CA)), 0.0), axis=1, keepdims=True)
        cnt[half * CA:(half + 1) * CA, :] = jnp.broadcast_to(column, (CA, CA))

    def bias_rows(k):
        pair_load(k).wait()

        def four(j, carry):
            first = k * PART_ROWS + 4 * j
            blocks = [jnp.transpose(pair[first + e]) for e in range(4)]
            for e in range(4):
                wide = blocks[e].astype(F32)
                s2[pl.ds(first + e, 1), :] = jnp.sum(wide * wide, axis=0, keepdims=True)
            square = jnp.concatenate(
                [jnp.concatenate(blocks[0:2], axis=1), jnp.concatenate(blocks[2:4], axis=1)], axis=0)
            sums = mm(gmat[...], square)
            for e in range(4):
                low, side = e // 2, slice((e % 2) * CA, (e % 2 + 1) * CA)
                bias[pl.ds(first + e, HEADS, stride=TQ), :] = sums[low * HEADS:(low + 1) * HEADS, side]
                s1[pl.ds(first + e, 1), :] = sums[2 * HEADS + low:2 * HEADS + low + 1, side]
            return carry

        lax.fori_loop(0, PART_ROWS // 4, four, 0, unroll=4)

    for k in range(FIRST_PARTS):
        bias_rows(k)

    a_all.wait_recv()
    own = rows_of(c, OWN)
    mean_own[...] = jnp.sum(abuf[...].astype(F32), axis=0) / cnt[own, :]
    means[own, :] = mean_own[...].astype(BF16)

    def k_copy(target):
        return remote(means.at[own], keymeans.at[key_slot], ksem, target, key_col)

    def b_copy(peer):
        return remote(means.at[own], means.at[own], bsem, r, peer)

    b_all = remote(means.at[other_rows], means.at[other_rows], bsem, r, next_col)
    each_target(lambda target: k_copy(target).start())
    each_peer(lambda peer: b_copy(peer).start())

    @pl.when(is_self)
    def _():
        keymeans[key_slot] = means[own, :]

    for k in range(FIRST_PARTS, PASS_PART):
        bias_rows(k)

    @pl.when(passes_on)
    def _():
        arrived = cond_copy(keycond, sibling)
        arrived.wait_recv()
        arrived.start()

    for k in range(PASS_PART, PAIR_PARTS):
        bias_rows(k)

    def normalize(hidden):
        center = hidden - jnp.mean(hidden, axis=-1, keepdims=True)
        spread = jnp.mean(center * center, axis=-1, keepdims=True)
        gain = jnp.concatenate([tgain[k:k + 1, :] for k in range(6)], axis=1)
        return (center * lax.rsqrt(spread + 1e-05) * gain).astype(BF16)

    for name in ("wagg", "cond", "tgain", "wq", "wkv"):
        loads[name].wait()
    @pl.when(holds)
    def _():
        keycond[...] = cond[rows_of(jnp.bitwise_and(c, 1), TK), :]

    @pl.when(jnp.logical_not(same_core))
    def _():
        cond_copy(keycond, sibling).wait_recv()

    from_sources(keymeans, ksem, lambda copy: copy.wait_recv())
    b_all.wait_recv()
    key_agg = mm(keymeans[...].reshape(TK, CA), wagg[...])
    aggv[...] = mm(means[...], wagg[...])
    key_rows = normalize(key_agg + keycond[...].astype(F32))
    for n in range(6):
        cols = slice(n * 256, (n + 1) * 256)
        kv[:, cols] = mm(key_rows, wkv[:, cols]).astype(BF16)
    for k in range(TQ // 64):
        at = slice(k * 64, (k + 1) * 64)
        normed[at, :] = normalize(aggv[at, :] + cond[at, :].astype(F32))
    for n in range(3):
        cols = slice(n * 256, (n + 1) * 256)
        qv[:, cols] = (mm(normed[...], wq[:, cols]) * (1.0 / math.sqrt(HD))).astype(BF16)

    def head_mask(first, width, head):
        lane = iota((1, width), 1) + first
        return jnp.where(jnp.logical_and(lane >= head * HD, lane < (head + 1) * HD), 1.0, 0.0).astype(BF16)

    windows = []
    for p in range(HEADS // 2):
        first = (2 * p * HD) // 128 * 128
        last = -(-((2 * p + 2) * HD) // 128) * 128
        windows.append((first, last - first))
        block = kv[:, first:last]
        for e in range(2):
            km[p, e * TK:(e + 1) * TK, 0:last - first] = block * head_mask(first, last - first, 2 * p + e)
    value_heads = []
    for n in range(3):
        heads = [h for h in range(HEADS) if h * HD < (n + 1) * 256 and (h + 1) * HD > n * 256]
        value_heads.append(heads)
        block = kv[:, D + n * 256:D + (n + 1) * 256]
        for slot, h in enumerate(heads):
            vm[n, slot * TK:(slot + 1) * TK, :] = block * head_mask(n * 256, 256, h)

    def c_copy(owner):
        return remote(wmsg.at[rows_of(owner, OWN)], cbuf.at[c], csem, r, owner)

    c_all = remote(wmsg.at[other_rows], cbuf.at[others], csem, r, next_col)
    def attend(start, size):
        at = pl.ds(pl.multiple_of(start, size), size)
        mean = s1[at, :] * (1.0 / CA)
        mean_high, mean_low = split(mean)
        mean_high = mean_high.astype(F32)
        mean_low = mean - mean_high
        var = (s2[at, :] * (1.0 / CA) - mean_high * mean_high) - mean_low * (mean_high + mean)
        rstd = lax.rsqrt(jnp.maximum(var, 0.0) + 1e-05)
        lane = iota((size, 128), 1)
        tops = jnp.zeros((size, 128), F32)
        for p in range(HEADS // 2):
            first, width = windows[p]
            scores = mm_nt(qv[at, first:first + width], km[p, :, 0:width])
            for e in range(2):
                h = 2 * p + e
                raw = bias[pl.ds(pl.multiple_of(h * TQ + start, size), size), :]
                sc = scores[:, e * TK:(e + 1) * TK] + (raw - mean * colsum[h:h + 1, :]) * rstd
                top = jnp.max(sc, axis=-1, keepdims=True)
                expo = jnp.exp(sc - top)
                probs[0:size, h * TK:(h + 1) * TK] = expo.astype(BF16)
                tops = jnp.where(lane == h, top, tops)
        for n in range(3):
            heads = value_heads[n]
            wide = probs[0:size, heads[0] * TK:(heads[-1] + 1) * TK]
            wmsg[at, n * 256:(n + 1) * 256] = mm(wide, vm[n]).astype(BF16)
        totals = mm(probs[0:size, :], head_ones[...])
        tops_high, tops_mid = split(tops)
        tops_low = (tops - tops_high.astype(F32) - tops_mid.astype(F32)).astype(BF16)
        totals_high, totals_low = split(totals)
        stats = tops_high.astype(F32)
        for place, piece in enumerate((tops_mid, tops_low, totals_high, totals_low)):
            stats = stats + pltpu.roll(piece.astype(F32), (place + 1) * HEADS, 1)
        wmsg[at, D:MSG] = stats.astype(BF16)

    plane = lax.shift_right_logical(c, 2)
    far = 2 * jnp.bitwise_xor(lax.shift_right_logical(c, 3), 1)
    near = jnp.bitwise_xor(plane, 1)
    attend(64 * far, 128)
    for k in range(4):
        for other_plane in (2, 3):
            c_copy(4 * jnp.bitwise_xor(plane, other_plane) + jnp.bitwise_and(c + k, 3)).start()
    attend(64 * near, 64)
    for k in range(4):
        c_copy(4 * near + jnp.bitwise_and(c + k, 3)).start()
    attend(64 * plane, 64)
    for k in (2, 1, 3):
        c_copy(4 * plane + jnp.bitwise_and(c + k, 3)).start()
    cbuf[c] = wmsg[own, :]
    mean_high, mean_low = split(mean_own[...])
    hidden_own = mm(mean_high, wagg[...]) + mm(mean_low, wagg[...]) + cond[own, :].astype(F32)
    spread_row = jnp.bitwise_and(iota((256, D), 0), 127)
    spread_col = iota((256, D), 1) - spread_row * HD
    expand[...] = jnp.where(jnp.logical_and(spread_col >= 0, spread_col < HD), 1.0, 0.0).astype(BF16)
    loads["wo"].wait()
    loads["wb"].wait()
    c_all.wait_recv()

    stat = cbuf[:, :, D:MSG].reshape(TQ, 128).astype(F32)
    def piece(k):
        return pltpu.roll(stat, 128 - k * HEADS, 1)

    tops = ((stat + piece(1)) + piece(2)).reshape(NCOL, OWN, 128)
    totals = (piece(3) + piece(4)).reshape(NCOL, OWN, 128)
    best = jnp.max(tops, axis=0, keepdims=True)
    scale = jnp.exp(tops - best)
    total = jnp.sum(scale * totals, axis=0, keepdims=True)
    valid = iota((1, 1, 128), 2) < HEADS
    total = jnp.where(valid, total, 1.0)
    factor = jnp.where(valid, scale / total, 0.0).reshape(TQ, 128)
    factor = jnp.concatenate(split(factor), axis=1)
    attn_parts = []
    for n in range(3):
        cols = slice(n * 256, (n + 1) * 256)
        wide = mm(factor, expand[:, cols])
        terms = cbuf[:, :, cols].astype(F32) * wide.reshape(NCOL, OWN, 256)
        attn_parts.append(jnp.sum(terms, axis=0).astype(BF16))
    attn = jnp.concatenate(attn_parts, axis=1)
    finished = (hidden_own + mm(attn, wo[...])).astype(BF16)

    tokbuf[c] = finished
    d_all = remote(tokbuf.at[others], tokbuf.at[others], dsem, r, next_col)
    each_peer(lambda peer: remote(tokbuf.at[c], tokbuf.at[c], dsem, r, peer).start())

    a_all.wait_send()
    b_all.wait_send()

    @pl.when(holds)
    def _():
        for k in range(4):
            cond_copy(held_cond, sibling).wait_send()

    @pl.when(passes_on)
    def _():
        cond_copy(keycond, sibling).wait_send()

    from_sources(keymeans, ksem, lambda copy: copy.wait_send())
    c_all.wait_send()

    d_all.wait_recv()
    token_store = pltpu.make_async_copy(tokbuf, token_out_h, osem.at[0])
    token_store.start()
    chosen = mm(pick[...], tokbuf[...].reshape(TQ, D)).astype(BF16)
    atomv[...] = (feats[...].astype(F32) + mm(chosen, wb[...])).astype(BF16)
    atom_store = pltpu.make_async_copy(atomv, atom_out_h, osem.at[1])
    atom_store.start()
    d_all.wait_send()
    token_store.wait()
    atom_store.wait()


def hand_over(token_in, atom_in, token_out, atom_out, sems):
    copies = [
        pltpu.make_async_copy(token_in, token_out, sems.at[0]),
        pltpu.make_async_copy(atom_in, atom_out, sems.at[1]),
    ]
    for copy in copies:
        copy.start()
    for copy in copies:
        copy.wait()


def local(
    atom_feats, atom_token, atom_counts, token_cond, pair, token_gain, pair_gain, w_bias, w_agg, w_query, w_keyval,
    w_out, w_back,
):
    any_space = pl.BlockSpec(memory_space=pl.ANY)
    hbm = pl.BlockSpec(memory_space=pltpu.HBM)
    vmem = pltpu.VMEM
    dma = pltpu.SemaphoreType.DMA
    scratch = [
        vmem((CA, CA), BF16), vmem((1, CA), jnp.int32), vmem((1, TQ), jnp.int32), vmem((TQ, D), BF16),
        vmem((TQ, TK, CA), BF16), vmem((6, 128), F32), vmem((1, CA), F32), vmem((HEADS, CA), BF16),
        vmem((CA, D), BF16), vmem((D, D), BF16), vmem((D, 2 * D), BF16), vmem((D, D), BF16), vmem((D, CA), BF16),
        vmem((3 * HEADS, 2 * CA), BF16), vmem((HEADS, CA), F32), vmem((HEADS * TQ, TK), F32), vmem((TQ, TK), F32),
        vmem((TQ, TK), F32), vmem((TQ, CA), BF16), vmem((NCOL, OWN, CA), BF16), vmem((TQ, CA), BF16), vmem((OWN, CA), F32),
        vmem((TQ, CA), F32),
        vmem((TQ, D), F32), vmem((TQ, D), BF16), vmem((TQ, D), BF16), vmem((TK, 2 * D), BF16),
        vmem((8, OWN, CA), BF16), vmem((TK, D), BF16),
        vmem((HEADS // 2, 2 * TK, 256), BF16), vmem((3, 6 * TK, 256), BF16), vmem((CHUNK, HEADS * TK), BF16),
        vmem((TQ, MSG), BF16), vmem((NCOL, OWN, MSG), BF16), vmem((256, D), BF16), vmem((NCOL, OWN, D), BF16),
        vmem((CA, TQ), BF16), vmem((CA, CA), BF16), vmem((HEADS * TK, 128), BF16),
        dma((13,)), dma((PAIR_PARTS,)), dma((2,)),
        *[dma((2,))] * 6,
    ]
    outs = pl.pallas_call(
        kernel,
        out_shape=(jax.ShapeDtypeStruct((NCOL, OWN, D), BF16), jax.ShapeDtypeStruct((CA, CA), BF16)),
        in_specs=[hbm] * 13,
        out_specs=(any_space, any_space),
        scratch_shapes=scratch,
        compiler_params=pltpu.CompilerParams(
            collective_id=0, has_side_effects=True, vmem_limit_bytes=40 * 1024 * 1024),
        name="diffusion_block",
    )(*[pltpu.with_memory_space_constraint(x, pltpu.HBM) for x in (
        atom_feats, atom_token.reshape(1, CA), atom_counts.reshape(1, TQ), token_cond, pair, token_gain.reshape(6, 128),
        pair_gain.reshape(1, CA), w_bias.T, w_agg, w_query, w_keyval, w_out, w_back,
    )])
    stored = pl.pallas_call(
        hand_over,
        out_shape=(jax.ShapeDtypeStruct((NCOL, OWN, D), BF16), jax.ShapeDtypeStruct((CA, CA), BF16)),
        in_specs=[any_space] * 2,
        out_specs=(any_space, any_space),
        scratch_shapes=[dma((2,))],
        compiler_params=pltpu.CompilerParams(vmem_limit_bytes=1024 * 1024),
        name="hand_over",
    )(*outs)
    return stored[0].reshape(TQ, D), stored[1]


def solution(mesh):
    placed = (
        P(("row", "col"), None), P(("row", "col")), P("row"), P("row", None), P("row", "col", None),
        P(), P(), P(), P(), P(), P(), P(), P(),
    )
    return jax.shard_map(
        local,
        mesh=mesh,
        in_specs=placed,
        out_specs=(P("row", None), P(("row", "col"), None)),
        check_vma=False,
    )
```

```python
import math

import jax
import jax.numpy as jnp
from jax import lax
from jax.experimental import pallas as pl
from jax.experimental.pallas import tpu as pltpu
from jax.sharding import PartitionSpec as P

D = 768
HEADS = 16
HD = 48
CA = 128
TQ = 256
TK = 128
NCOL = 16
NROW = 8
OWN = TQ // NCOL
MSG = D + 128
CHUNK = 64
PAIR_PARTS = 8
PART_ROWS = TQ // PAIR_PARTS
FIRST_PARTS = 3
PASS_PART = 6
MESH = pl.DeviceIdType.MESH
F32 = jnp.float32
BF16 = jnp.bfloat16


def mm(a, b):
    return jnp.dot(a, b, preferred_element_type=F32)


def mm_nt(a, b):
    return lax.dot_general(a, b, (((1,), (1,)), ((), ())), preferred_element_type=F32)


def iota(shape, axis):
    return lax.broadcasted_iota(jnp.int32, shape, axis)


def split(x):
    high = x.astype(BF16)
    low = (x - high.astype(F32)).astype(BF16)
    return high, low


def rows_of(index, size):
    return pl.ds(pl.multiple_of(index * size, size), size)


def kernel(
    feats_h, tok_h, counts_h, cond_h, pair_h, tgain_h, pgain_h, wbias_h, wagg_h, wq_h, wkv_h, wo_h, wb_h,
    token_out_h, atom_out_h,
    feats, tok, counts, cond, pair, tgain, pgain, wbias, wagg, wq, wkv, wo, wb,
    gmat, colsum, bias, s1, s2, part, abuf, means, mean_own, cnt, qv, kv, keymeans, keycond,
    km, vm, probs, wmsg, cbuf, expand, tokbuf, pick, atomv, head_ones,
    lsem, psem, osem, asem, bsem, ksem, csem, qsem, dsem,
):
    r = lax.axis_index("row")
    c = lax.axis_index("col")
    key_col = 2 * r + lax.shift_right_logical(c, 3)
    key_slot = jnp.bitwise_and(c, 7)
    src_row = lax.shift_right_logical(c, 1)
    src_col = 8 * jnp.bitwise_and(c, 1)
    is_self = c == key_col
    other = jnp.logical_not(is_self)
    holds = r == src_row
    same_core = jnp.bitwise_and(r, 1) == jnp.bitwise_and(src_row, 1)
    sibling = jnp.bitwise_xor(r, 1)
    passes_on = jnp.logical_and(same_core, jnp.logical_not(holds))

    def col_at(offset):
        return jnp.bitwise_and(c + offset, NCOL - 1)

    next_col = col_at(1)

    def local(i, src, dst):
        return pltpu.make_async_copy(src, dst, lsem.at[i])

    loads = {
        "feats": local(0, feats_h, feats),
        "tok": local(1, tok_h, tok),
        "counts": local(2, counts_h, counts),
        "wbias": local(3, wbias_h, wbias),
        "pgain": local(4, pgain_h, pgain),
        "wagg": local(5, wagg_h, wagg),
        "cond": local(7, cond_h, cond),
        "tgain": local(8, tgain_h, tgain),
        "wq": local(9, wq_h, wq),
        "wkv": local(10, wkv_h, wkv),
        "wo": local(11, wo_h, wo),
        "wb": local(12, wb_h, wb),
    }

    def pair_load(k):
        at = pl.ds(k * PART_ROWS, PART_ROWS)
        return pltpu.make_async_copy(pair_h.at[at], pair.at[at], psem.at[k])

    for name in ("feats", "tok", "counts", "wbias", "pgain"):
        loads[name].start()

    barrier = pltpu.get_barrier_semaphore()

    def greet(row, col):
        pl.semaphore_signal(barrier, inc=1, device_id=(row, col), device_id_type=MESH)

    for k in range(1, NCOL):
        greet(r, col_at(k))
    for k in range(1, 8):
        greet(src_row, src_col + jnp.bitwise_and(c + k, 7))

    @pl.when(other)
    def _():
        greet(src_row, src_col + key_slot)

    @pl.when(jnp.logical_not(holds))
    def _():
        greet(jnp.where(same_core, src_row, sibling), c)

    for k in range(FIRST_PARTS):
        pair_load(k).start()

    loads["feats"].wait()
    loads["tok"].wait()
    here = tok[...] - r * TQ
    member = jnp.where(iota((TQ, CA), 0) == here, 1.0, 0.0).astype(BF16)
    part[...] = mm(member, feats[...]).astype(BF16)

    pl.semaphore_wait(
        barrier,
        NCOL - 1 + 8 - is_self.astype(jnp.int32) + 4 * holds.astype(jnp.int32) + passes_on.astype(jnp.int32))

    def remote(src, dst, sems, row, col):
        return pltpu.make_async_remote_copy(
            src_ref=src, dst_ref=dst, send_sem=sems.at[0], recv_sem=sems.at[1],
            device_id=(row, col), device_id_type=MESH)

    others = pl.ds(0, NCOL - 1)
    other_rows = pl.ds(0, (NCOL - 1) * OWN)

    def a_copy(peer):
        return remote(part.at[rows_of(peer, OWN)], abuf.at[c], asem, r, peer)

    a_all = remote(part.at[other_rows], abuf.at[others], asem, r, next_col)

    def each_peer(action):
        for k in (8, 9, 10, 11, 12, 13, 14, 15, 1, 2, 3, 4, 5, 6, 7):
            action(col_at(k))

    each_peer(lambda peer: a_copy(peer).start())
    for name in ("wagg", "cond", "tgain"):
        loads[name].start()
    for k in range(FIRST_PARTS, PAIR_PARTS):
        pair_load(k).start()
    for name in ("wq", "wkv", "wo", "wb"):
        loads[name].start()

    def each_target(action):
        for k in range(1, NROW):
            action(jnp.bitwise_and(r + k, NROW - 1))

        @pl.when(other)
        def _():
            action(r)

    def from_sources(buffer, sems, action):
        for count in (7, 8):
            @pl.when(is_self == (count == 7))
            def _():
                action(remote(buffer.at[pl.ds(0, count)], buffer.at[pl.ds(0, count)], sems, r, next_col))

    held_cond = cond_h.at[rows_of(jnp.bitwise_and(c, 1), TK)]

    def cond_copy(source, row):
        return remote(source, keycond, qsem, row, c)

    @pl.when(holds)
    def _():
        for k in (4, 2, 6):
            cond_copy(held_cond, jnp.bitwise_and(r + k, NROW - 1)).start()
        cond_copy(held_cond, sibling).start()

    abuf[c] = part[rows_of(c, OWN), :]

    for h in range(HEADS):
        head_ones[h * TK:(h + 1) * TK, :] = jnp.where(iota((TK, 128), 1) == h, 1.0, 0.0).astype(BF16)
    eye = iota((CA, CA), 0) == iota((CA, CA), 1)
    eye_b = jnp.where(eye, 1.0, 0.0).astype(BF16)
    pick[...] = mm_nt(eye_b, member).astype(BF16)
    loads["wbias"].wait()
    loads["pgain"].wait()
    gain_t = (wbias[...].astype(F32) * pgain[...]).astype(BF16)
    none = jnp.zeros((HEADS, CA), BF16)
    place = iota((HEADS, CA), 0)
    ones_left = jnp.where(place == 0, 1.0, 0.0).astype(BF16)
    ones_right = jnp.where(place == 1, 1.0, 0.0).astype(BF16)
    gmat[:, 0:CA] = jnp.concatenate([gain_t, none, ones_left], axis=0)
    gmat[:, CA:2 * CA] = jnp.concatenate([none, gain_t, ones_right], axis=0)
    colsum[...] = jnp.broadcast_to(jnp.sum(gain_t.astype(F32), axis=1, keepdims=True), (HEADS, CA))
    loads["counts"].wait()
    for half in range(2):
        line = counts[:, half * CA:(half + 1) * CA].astype(F32)
        column = jnp.sum(jnp.where(eye, jnp.broadcast_to(line, (CA, CA)), 0.0), axis=1, keepdims=True)
        cnt[half * CA:(half + 1) * CA, :] = jnp.broadcast_to(column, (CA, CA))

    def bias_rows(k):
        pair_load(k).wait()

        def four(j, carry):
            first = k * PART_ROWS + 4 * j
            blocks = [jnp.transpose(pair[first + e]) for e in range(4)]
            for e in range(4):
                wide = blocks[e].astype(F32)
                s2[pl.ds(first + e, 1), :] = jnp.sum(wide * wide, axis=0, keepdims=True)
            square = jnp.concatenate(
                [jnp.concatenate(blocks[0:2], axis=1), jnp.concatenate(blocks[2:4], axis=1)], axis=0)
            sums = mm(gmat[...], square)
            for e in range(4):
                low, side = e // 2, slice((e % 2) * CA, (e % 2 + 1) * CA)
                bias[pl.ds(first + e, HEADS, stride=TQ), :] = sums[low * HEADS:(low + 1) * HEADS, side]
                s1[pl.ds(first + e, 1), :] = sums[2 * HEADS + low:2 * HEADS + low + 1, side]
            return carry

        lax.fori_loop(0, PART_ROWS // 4, four, 0, unroll=4)

    for k in range(FIRST_PARTS):
        bias_rows(k)

    a_all.wait_recv()
    own = rows_of(c, OWN)
    mean_own[...] = jnp.sum(abuf[...].astype(F32), axis=0) / cnt[own, :]
    means[own, :] = mean_own[...].astype(BF16)

    def k_copy(target):
        return remote(means.at[own], keymeans.at[key_slot], ksem, target, key_col)

    def b_copy(peer):
        return remote(means.at[own], means.at[own], bsem, r, peer)

    b_all = remote(means.at[other_rows], means.at[other_rows], bsem, r, next_col)
    each_target(lambda target: k_copy(target).start())
    each_peer(lambda peer: b_copy(peer).start())

    @pl.when(is_self)
    def _():
        keymeans[key_slot] = means[own, :]

    for k in range(FIRST_PARTS, PASS_PART):
        bias_rows(k)

    @pl.when(passes_on)
    def _():
        arrived = cond_copy(keycond, sibling)
        arrived.wait_recv()
        arrived.start()

    for k in range(PASS_PART, PAIR_PARTS):
        bias_rows(k)

    def normalize(hidden):
        center = hidden - jnp.mean(hidden, axis=-1, keepdims=True)
        spread = jnp.mean(center * center, axis=-1, keepdims=True)
        gain = jnp.concatenate([tgain[k:k + 1, :] for k in range(6)], axis=1)
        return (center * lax.rsqrt(spread + 1e-05) * gain).astype(BF16)

    for name in ("wagg", "cond", "tgain", "wq", "wkv"):
        loads[name].wait()
    @pl.when(holds)
    def _():
        keycond[...] = cond[rows_of(jnp.bitwise_and(c, 1), TK), :]

    @pl.when(jnp.logical_not(same_core))
    def _():
        cond_copy(keycond, sibling).wait_recv()

    from_sources(keymeans, ksem, lambda copy: copy.wait_recv())
    b_all.wait_recv()
    key_agg = mm(keymeans[...].reshape(TK, CA), wagg[...])
    key_rows = normalize(key_agg + keycond[...].astype(F32))
    for n in range(6):
        cols = slice(n * 256, (n + 1) * 256)
        kv[:, cols] = mm(key_rows, wkv[:, cols]).astype(BF16)

    def query_rows(plane):
        at = rows_of(plane, CHUNK)
        hidden = mm(means[at, :], wagg[...]) + cond[at, :].astype(F32)
        qv[at, :] = (mm(normalize(hidden), wq[...]) * (1.0 / math.sqrt(HD))).astype(BF16)

    def head_mask(first, width, head):
        lane = iota((1, width), 1) + first
        return jnp.where(jnp.logical_and(lane >= head * HD, lane < (head + 1) * HD), 1.0, 0.0).astype(BF16)

    windows = []
    for p in range(HEADS // 2):
        first = (2 * p * HD) // 128 * 128
        last = -(-((2 * p + 2) * HD) // 128) * 128
        windows.append((first, last - first))
        block = kv[:, first:last]
        for e in range(2):
            km[p, e * TK:(e + 1) * TK, 0:last - first] = block * head_mask(first, last - first, 2 * p + e)
    value_heads = []
    for n in range(3):
        heads = [h for h in range(HEADS) if h * HD < (n + 1) * 256 and (h + 1) * HD > n * 256]
        value_heads.append(heads)
        block = kv[:, D + n * 256:D + (n + 1) * 256]
        for slot, h in enumerate(heads):
            vm[n, slot * TK:(slot + 1) * TK, :] = block * head_mask(n * 256, 256, h)

    def c_copy(owner):
        return remote(wmsg.at[rows_of(owner, OWN)], cbuf.at[c], csem, r, owner)

    c_all = remote(wmsg.at[other_rows], cbuf.at[others], csem, r, next_col)
    def attend(plane, probs):
        start, size = plane * CHUNK, CHUNK
        at = rows_of(plane, CHUNK)
        mean = s1[at, :] * (1.0 / CA)
        mean_high, mean_low = split(mean)
        mean_high = mean_high.astype(F32)
        mean_low = mean - mean_high
        var = (s2[at, :] * (1.0 / CA) - mean_high * mean_high) - mean_low * (mean_high + mean)
        rstd = lax.rsqrt(jnp.maximum(var, 0.0) + 1e-05)
        lane = iota((size, 128), 1)
        tops = jnp.zeros((size, 128), F32)
        for p in range(HEADS // 2):
            first, width = windows[p]
            scores = mm_nt(qv[at, first:first + width], km[p, :, 0:width])
            for e in range(2):
                h = 2 * p + e
                raw = bias[pl.ds(pl.multiple_of(h * TQ + start, size), size), :]
                sc = scores[:, e * TK:(e + 1) * TK] + (raw - mean * colsum[h:h + 1, :]) * rstd
                top = jnp.max(sc, axis=-1, keepdims=True)
                expo = jnp.exp(sc - top)
                probs[:, h * TK:(h + 1) * TK] = expo.astype(BF16)
                tops = jnp.where(lane == h, top, tops)
        for n in range(3):
            heads = value_heads[n]
            wide = probs[:, heads[0] * TK:(heads[-1] + 1) * TK]
            wmsg[at, n * 256:(n + 1) * 256] = mm(wide, vm[n]).astype(BF16)
        totals = mm(probs[:, :], head_ones[...])
        tops_high, tops_mid = split(tops)
        tops_low = (tops - tops_high.astype(F32) - tops_mid.astype(F32)).astype(BF16)
        totals_high, totals_low = split(totals)
        stats = tops_high.astype(F32)
        for place, piece in enumerate((tops_mid, tops_low, totals_high, totals_low)):
            stats = stats + pltpu.roll(piece.astype(F32), (place + 1) * HEADS, 1)
        wmsg[at, D:MSG] = stats.astype(BF16)

    plane = lax.shift_right_logical(c, 2)
    planes = [jnp.bitwise_xor(plane, k) for k in (2, 3, 1, 0)]
    query_rows(planes[0])
    for n, target in enumerate(planes):
        if n < 3:
            query_rows(planes[n + 1])
        attend(target, probs.at[n % 2])
        for k in (2, 1, 3, 0) if n < 3 else (2, 1, 3):
            c_copy(4 * target + jnp.bitwise_and(c + k, 3)).start()
    cbuf[c] = wmsg[own, :]
    mean_high, mean_low = split(mean_own[...])
    hidden_own = mm(mean_high, wagg[...]) + mm(mean_low, wagg[...]) + cond[own, :].astype(F32)
    spread_row = jnp.bitwise_and(iota((256, D), 0), 127)
    spread_col = iota((256, D), 1) - spread_row * HD
    expand[...] = jnp.where(jnp.logical_and(spread_col >= 0, spread_col < HD), 1.0, 0.0).astype(BF16)
    loads["wo"].wait()
    loads["wb"].wait()
    c_all.wait_recv()

    stat = cbuf[:, :, D:MSG].reshape(TQ, 128).astype(F32)
    def piece(k):
        return pltpu.roll(stat, 128 - k * HEADS, 1)

    tops = ((stat + piece(1)) + piece(2)).reshape(NCOL, OWN, 128)
    totals = (piece(3) + piece(4)).reshape(NCOL, OWN, 128)
    best = jnp.max(tops, axis=0, keepdims=True)
    scale = jnp.exp(tops - best)
    total = jnp.sum(scale * totals, axis=0, keepdims=True)
    valid = iota((1, 1, 128), 2) < HEADS
    total = jnp.where(valid, total, 1.0)
    factor = jnp.where(valid, scale / total, 0.0).reshape(TQ, 128)
    factor = jnp.concatenate(split(factor), axis=1)
    attn_parts = []
    for n in range(3):
        cols = slice(n * 256, (n + 1) * 256)
        wide = mm(factor, expand[:, cols])
        terms = cbuf[:, :, cols].astype(F32) * wide.reshape(NCOL, OWN, 256)
        attn_parts.append(jnp.sum(terms, axis=0).astype(BF16))
    attn = jnp.concatenate(attn_parts, axis=1)
    finished = (hidden_own + mm(attn, wo[...])).astype(BF16)

    tokbuf[c] = finished
    d_all = remote(tokbuf.at[others], tokbuf.at[others], dsem, r, next_col)
    each_peer(lambda peer: remote(tokbuf.at[c], tokbuf.at[c], dsem, r, peer).start())

    a_all.wait_send()
    b_all.wait_send()

    @pl.when(holds)
    def _():
        for k in range(4):
            cond_copy(held_cond, sibling).wait_send()

    @pl.when(passes_on)
    def _():
        cond_copy(keycond, sibling).wait_send()

    from_sources(keymeans, ksem, lambda copy: copy.wait_send())
    c_all.wait_send()

    d_all.wait_recv()
    token_store = pltpu.make_async_copy(tokbuf, token_out_h, osem.at[0])
    token_store.start()
    chosen = mm(pick[...], tokbuf[...].reshape(TQ, D)).astype(BF16)
    atomv[...] = (feats[...].astype(F32) + mm(chosen, wb[...])).astype(BF16)
    atom_store = pltpu.make_async_copy(atomv, atom_out_h, osem.at[1])
    atom_store.start()
    d_all.wait_send()
    token_store.wait()
    atom_store.wait()


def hand_over(token_in, atom_in, token_out, atom_out, sems):
    copies = [
        pltpu.make_async_copy(token_in, token_out, sems.at[0]),
        pltpu.make_async_copy(atom_in, atom_out, sems.at[1]),
    ]
    for copy in copies:
        copy.start()
    for copy in copies:
        copy.wait()


def local(
    atom_feats, atom_token, atom_counts, token_cond, pair, token_gain, pair_gain, w_bias, w_agg, w_query, w_keyval,
    w_out, w_back,
):
    any_space = pl.BlockSpec(memory_space=pl.ANY)
    hbm = pl.BlockSpec(memory_space=pltpu.HBM)
    vmem = pltpu.VMEM
    dma = pltpu.SemaphoreType.DMA
    scratch = [
        vmem((CA, CA), BF16), vmem((1, CA), jnp.int32), vmem((1, TQ), jnp.int32), vmem((TQ, D), BF16),
        vmem((TQ, TK, CA), BF16), vmem((6, 128), F32), vmem((1, CA), F32), vmem((HEADS, CA), BF16),
        vmem((CA, D), BF16), vmem((D, D), BF16), vmem((D, 2 * D), BF16), vmem((D, D), BF16), vmem((D, CA), BF16),
        vmem((3 * HEADS, 2 * CA), BF16), vmem((HEADS, CA), F32), vmem((HEADS * TQ, TK), F32), vmem((TQ, TK), F32),
        vmem((TQ, TK), F32), vmem((TQ, CA), BF16), vmem((NCOL, OWN, CA), BF16), vmem((TQ, CA), BF16), vmem((OWN, CA), F32),
        vmem((TQ, CA), F32),
        vmem((TQ, D), BF16), vmem((TK, 2 * D), BF16),
        vmem((8, OWN, CA), BF16), vmem((TK, D), BF16),
        vmem((HEADS // 2, 2 * TK, 256), BF16), vmem((3, 6 * TK, 256), BF16), vmem((2, CHUNK, HEADS * TK), BF16),
        vmem((TQ, MSG), BF16), vmem((NCOL, OWN, MSG), BF16), vmem((256, D), BF16), vmem((NCOL, OWN, D), BF16),
        vmem((CA, TQ), BF16), vmem((CA, CA), BF16), vmem((HEADS * TK, 128), BF16),
        dma((13,)), dma((PAIR_PARTS,)), dma((2,)),
        *[dma((2,))] * 6,
    ]
    outs = pl.pallas_call(
        kernel,
        out_shape=(jax.ShapeDtypeStruct((NCOL, OWN, D), BF16), jax.ShapeDtypeStruct((CA, CA), BF16)),
        in_specs=[hbm] * 13,
        out_specs=(any_space, any_space),
        scratch_shapes=scratch,
        compiler_params=pltpu.CompilerParams(
            collective_id=0, has_side_effects=True, vmem_limit_bytes=40 * 1024 * 1024),
        name="diffusion_block",
    )(*[pltpu.with_memory_space_constraint(x, pltpu.HBM) for x in (
        atom_feats, atom_token.reshape(1, CA), atom_counts.reshape(1, TQ), token_cond, pair, token_gain.reshape(6, 128),
        pair_gain.reshape(1, CA), w_bias.T, w_agg, w_query, w_keyval, w_out, w_back,
    )])
    stored = pl.pallas_call(
        hand_over,
        out_shape=(jax.ShapeDtypeStruct((NCOL, OWN, D), BF16), jax.ShapeDtypeStruct((CA, CA), BF16)),
        in_specs=[any_space] * 2,
        out_specs=(any_space, any_space),
        scratch_shapes=[dma((2,))],
        compiler_params=pltpu.CompilerParams(vmem_limit_bytes=1024 * 1024),
        name="hand_over",
    )(*outs)
    return stored[0].reshape(TQ, D), stored[1]


def solution(mesh):
    placed = (
        P(("row", "col"), None), P(("row", "col")), P("row"), P("row", None), P("row", "col", None),
        P(), P(), P(), P(), P(), P(), P(), P(),
    )
    return jax.shard_map(
        local,
        mesh=mesh,
        in_specs=placed,
        out_specs=(P("row", None), P(("row", "col"), None)),
        check_vma=False,
    )
```

```python
import math

import jax
import jax.numpy as jnp
from jax import lax
from jax.experimental import pallas as pl
from jax.experimental.pallas import tpu as pltpu
from jax.sharding import PartitionSpec as P

D = 768
HEADS = 16
HD = 48
CA = 128
TQ = 256
TK = 128
NCOL = 16
NROW = 8
OWN = TQ // NCOL
MSG = D + 128
CHUNK = 128
PAIR_PARTS = 8
PART_ROWS = TQ // PAIR_PARTS
FIRST_PARTS = 4
PASS_PART = 6
MESH = pl.DeviceIdType.MESH
F32 = jnp.float32
BF16 = jnp.bfloat16


def mm(a, b):
    return jnp.dot(a, b, preferred_element_type=F32)


def mm_nt(a, b):
    return lax.dot_general(a, b, (((1,), (1,)), ((), ())), preferred_element_type=F32)


def iota(shape, axis):
    return lax.broadcasted_iota(jnp.int32, shape, axis)


def split(x):
    high = x.astype(BF16)
    low = (x - high.astype(F32)).astype(BF16)
    return high, low


def rows_of(index, size):
    return pl.ds(pl.multiple_of(index * size, size), size)


def kernel(
    feats_h, tok_h, counts_h, cond_h, pair_h, tgain_h, pgain_h, wbias_h, wagg_h, wq_h, wkv_h, wo_h, wb_h,
    token_out_h, atom_out_h,
    feats, tok, counts, cond, pair, tgain, pgain, wbias, wagg, wq, wkv, wo, wb,
    gmat, colsum, bias, s1, s2, part, abuf, means, mean_own, cnt, aggv, normed, qv, kv, keymeans, keycond,
    km, vm, probs, wmsg, cbuf, expand, tokbuf, pick, atomv,
    lsem, psem, osem, asem, bsem, ksem, csem, qsem, dsem,
):
    r = lax.axis_index("row")
    c = lax.axis_index("col")
    key_col = 2 * r + lax.shift_right_logical(c, 3)
    key_slot = jnp.bitwise_and(c, 7)
    src_row = lax.shift_right_logical(c, 1)
    src_col = 8 * jnp.bitwise_and(c, 1)
    is_self = c == key_col
    other = jnp.logical_not(is_self)
    holds = r == src_row
    same_core = jnp.bitwise_and(r, 1) == jnp.bitwise_and(src_row, 1)
    sibling = jnp.bitwise_xor(r, 1)
    passes_on = jnp.logical_and(same_core, jnp.logical_not(holds))

    def col_at(offset):
        return jnp.bitwise_and(c + offset, NCOL - 1)

    next_col = col_at(1)

    def local(i, src, dst):
        return pltpu.make_async_copy(src, dst, lsem.at[i])

    loads = {
        "feats": local(0, feats_h, feats),
        "tok": local(1, tok_h, tok),
        "counts": local(2, counts_h, counts),
        "wbias": local(3, wbias_h, wbias),
        "pgain": local(4, pgain_h, pgain),
        "wagg": local(5, wagg_h, wagg),
        "cond": local(7, cond_h, cond),
        "tgain": local(8, tgain_h, tgain),
        "wq": local(9, wq_h, wq),
        "wkv": local(10, wkv_h, wkv),
        "wo": local(11, wo_h, wo),
        "wb": local(12, wb_h, wb),
    }

    def pair_load(k):
        at = pl.ds(k * PART_ROWS, PART_ROWS)
        return pltpu.make_async_copy(pair_h.at[at], pair.at[at], psem.at[k])

    for name in ("feats", "tok", "counts", "wbias", "pgain"):
        loads[name].start()

    barrier = pltpu.get_barrier_semaphore()

    def greet(row, col):
        pl.semaphore_signal(barrier, inc=1, device_id=(row, col), device_id_type=MESH)

    for k in range(1, NCOL):
        greet(r, col_at(k))
    for k in range(1, 8):
        greet(src_row, src_col + jnp.bitwise_and(c + k, 7))

    @pl.when(other)
    def _():
        greet(src_row, src_col + key_slot)

    @pl.when(jnp.logical_not(holds))
    def _():
        greet(jnp.where(same_core, src_row, sibling), c)

    for k in range(3):
        pair_load(k).start()

    loads["feats"].wait()
    loads["tok"].wait()
    here = tok[...] - r * TQ
    member = jnp.where(iota((TQ, CA), 0) == here, 1.0, 0.0).astype(BF16)
    part[...] = mm(member, feats[...]).astype(BF16)

    pl.semaphore_wait(
        barrier,
        NCOL - 1 + 8 - is_self.astype(jnp.int32) + 4 * holds.astype(jnp.int32) + passes_on.astype(jnp.int32))

    def remote(src, dst, sems, row, col):
        return pltpu.make_async_remote_copy(
            src_ref=src, dst_ref=dst, send_sem=sems.at[0], recv_sem=sems.at[1],
            device_id=(row, col), device_id_type=MESH)

    others = pl.ds(0, NCOL - 1)
    other_rows = pl.ds(0, (NCOL - 1) * OWN)

    def a_copy(peer):
        return remote(part.at[rows_of(peer, OWN)], abuf.at[c], asem, r, peer)

    a_all = remote(part.at[other_rows], abuf.at[others], asem, r, next_col)

    def each_peer(action):
        for k in (8, 9, 10, 11, 12, 13, 14, 15, 1, 2, 3, 4, 5, 6, 7):
            action(col_at(k))

    each_peer(lambda peer: a_copy(peer).start())
    for name in ("wagg", "cond", "tgain"):
        loads[name].start()
    for k in range(3, PAIR_PARTS):
        pair_load(k).start()
    for name in ("wq", "wkv", "wo", "wb"):
        loads[name].start()

    def each_target(action):
        for k in range(1, NROW):
            action(jnp.bitwise_and(r + k, NROW - 1))

        @pl.when(other)
        def _():
            action(r)

    def from_sources(buffer, sems, action):
        for count in (7, 8):
            @pl.when(is_self == (count == 7))
            def _():
                action(remote(buffer.at[pl.ds(0, count)], buffer.at[pl.ds(0, count)], sems, r, next_col))

    held_cond = cond_h.at[rows_of(jnp.bitwise_and(c, 1), TK)]

    def cond_copy(source, row):
        return remote(source, keycond, qsem, row, c)

    @pl.when(holds)
    def _():
        for k in (4, 2, 6):
            cond_copy(held_cond, jnp.bitwise_and(r + k, NROW - 1)).start()
        cond_copy(held_cond, sibling).start()

    abuf[c] = part[rows_of(c, OWN), :]

    eye = iota((CA, CA), 0) == iota((CA, CA), 1)
    eye_b = jnp.where(eye, 1.0, 0.0).astype(BF16)
    pick[...] = mm_nt(eye_b, member).astype(BF16)
    loads["wbias"].wait()
    loads["pgain"].wait()
    gain_t = (wbias[...].astype(F32) * pgain[...]).astype(BF16)
    none = jnp.zeros((HEADS, CA), BF16)
    place = iota((HEADS, CA), 0)
    ones_left = jnp.where(place == 0, 1.0, 0.0).astype(BF16)
    ones_right = jnp.where(place == 1, 1.0, 0.0).astype(BF16)
    gmat[:, 0:CA] = jnp.concatenate([gain_t, none, ones_left], axis=0)
    gmat[:, CA:2 * CA] = jnp.concatenate([none, gain_t, ones_right], axis=0)
    colsum[...] = jnp.broadcast_to(jnp.sum(gain_t.astype(F32), axis=1, keepdims=True), (HEADS, CA))
    loads["counts"].wait()
    for half in range(2):
        line = counts[:, half * CA:(half + 1) * CA].astype(F32)
        column = jnp.sum(jnp.where(eye, jnp.broadcast_to(line, (CA, CA)), 0.0), axis=1, keepdims=True)
        cnt[half * CA:(half + 1) * CA, :] = jnp.broadcast_to(column, (CA, CA))

    def bias_rows(k):
        pair_load(k).wait()

        def four(j, carry):
            first = k * PART_ROWS + 4 * j
            blocks = [jnp.transpose(pair[first + e]) for e in range(4)]
            for e in range(4):
                wide = blocks[e].astype(F32)
                s2[pl.ds(first + e, 1), :] = jnp.sum(wide * wide, axis=0, keepdims=True)
            square = jnp.concatenate(
                [jnp.concatenate(blocks[0:2], axis=1), jnp.concatenate(blocks[2:4], axis=1)], axis=0)
            sums = mm(gmat[...], square)
            for e in range(4):
                low, side = e // 2, slice((e % 2) * CA, (e % 2 + 1) * CA)
                bias[pl.ds(first + e, HEADS, stride=TQ), :] = sums[low * HEADS:(low + 1) * HEADS, side]
                s1[pl.ds(first + e, 1), :] = sums[2 * HEADS + low:2 * HEADS + low + 1, side]
            return carry

        lax.fori_loop(0, PART_ROWS // 4, four, 0, unroll=8)

    for k in range(FIRST_PARTS):
        bias_rows(k)

    a_all.wait_recv()
    own = rows_of(c, OWN)
    mean_own[...] = jnp.sum(abuf[...].astype(F32), axis=0) / cnt[own, :]
    means[own, :] = mean_own[...].astype(BF16)

    def k_copy(target):
        return remote(means.at[own], keymeans.at[key_slot], ksem, target, key_col)

    def b_copy(peer):
        return remote(means.at[own], means.at[own], bsem, r, peer)

    b_all = remote(means.at[other_rows], means.at[other_rows], bsem, r, next_col)
    each_target(lambda target: k_copy(target).start())
    each_peer(lambda peer: b_copy(peer).start())

    @pl.when(is_self)
    def _():
        keymeans[key_slot] = means[own, :]

    for k in range(FIRST_PARTS, PASS_PART):
        bias_rows(k)

    @pl.when(passes_on)
    def _():
        arrived = cond_copy(keycond, sibling)
        arrived.wait_recv()
        arrived.start()

    for k in range(PASS_PART, PAIR_PARTS):
        bias_rows(k)

    def normalize(hidden):
        center = hidden - jnp.mean(hidden, axis=-1, keepdims=True)
        spread = jnp.mean(center * center, axis=-1, keepdims=True)
        gain = jnp.concatenate([tgain[k:k + 1, :] for k in range(6)], axis=1)
        return (center * lax.rsqrt(spread + 1e-05) * gain).astype(BF16)

    for name in ("wagg", "cond", "tgain", "wq", "wkv"):
        loads[name].wait()
    @pl.when(holds)
    def _():
        keycond[...] = cond[rows_of(jnp.bitwise_and(c, 1), TK), :]

    @pl.when(jnp.logical_not(same_core))
    def _():
        cond_copy(keycond, sibling).wait_recv()

    from_sources(keymeans, ksem, lambda copy: copy.wait_recv())
    b_all.wait_recv()
    key_agg = mm(keymeans[...].reshape(TK, CA), wagg[...])
    aggv[...] = mm(means[...], wagg[...])
    key_rows = normalize(key_agg + keycond[...].astype(F32))
    for n in range(6):
        cols = slice(n * 256, (n + 1) * 256)
        kv[:, cols] = mm(key_rows, wkv[:, cols]).astype(BF16)
    for k in range(TQ // 64):
        at = slice(k * 64, (k + 1) * 64)
        normed[at, :] = normalize(aggv[at, :] + cond[at, :].astype(F32))
    for n in range(3):
        cols = slice(n * 256, (n + 1) * 256)
        qv[:, cols] = (mm(normed[...], wq[:, cols]) * (1.0 / math.sqrt(HD))).astype(BF16)

    def head_mask(first, width, head):
        lane = iota((1, width), 1) + first
        return jnp.where(jnp.logical_and(lane >= head * HD, lane < (head + 1) * HD), 1.0, 0.0).astype(BF16)

    windows = []
    for p in range(HEADS // 2):
        first = (2 * p * HD) // 128 * 128
        last = -(-((2 * p + 2) * HD) // 128) * 128
        windows.append((first, last - first))
        block = kv[:, first:last]
        for e in range(2):
            km[p, e * TK:(e + 1) * TK, 0:last - first] = block * head_mask(first, last - first, 2 * p + e)
    value_heads = []
    for n in range(3):
        heads = [h for h in range(HEADS) if h * HD < (n + 1) * 256 and (h + 1) * HD > n * 256]
        value_heads.append(heads)
        block = kv[:, D + n * 256:D + (n + 1) * 256]
        for slot, h in enumerate(heads):
            vm[n, slot * TK:(slot + 1) * TK, :] = block * head_mask(n * 256, 256, h)

    def c_copy(owner):
        return remote(wmsg.at[rows_of(owner, OWN)], cbuf.at[c], csem, r, owner)

    c_all = remote(wmsg.at[other_rows], cbuf.at[others], csem, r, next_col)
    owners = CHUNK // OWN
    chunks = TQ // CHUNK

    def attend(step):
        chunk = jnp.bitwise_and(lax.shift_right_logical(c, 3) + step, chunks - 1)
        at = rows_of(chunk, CHUNK)
        mean = s1[at, :] * (1.0 / CA)
        mean_high, mean_low = split(mean)
        mean_high = mean_high.astype(F32)
        mean_low = mean - mean_high
        var = (s2[at, :] * (1.0 / CA) - mean_high * mean_high) - mean_low * (mean_high + mean)
        rstd = lax.rsqrt(jnp.maximum(var, 0.0) + 1e-05)
        lane = iota((CHUNK, 128), 1)
        tops = jnp.zeros((CHUNK, 128), F32)
        totals = jnp.zeros((CHUNK, 128), F32)
        for p in range(HEADS // 2):
            first, width = windows[p]
            scores = mm_nt(qv[at, first:first + width], km[p, :, 0:width])
            for e in range(2):
                h = 2 * p + e
                raw = bias[pl.ds(pl.multiple_of(h * TQ + chunk * CHUNK, CHUNK), CHUNK), :]
                sc = scores[:, e * TK:(e + 1) * TK] + (raw - mean * colsum[h:h + 1, :]) * rstd
                top = jnp.max(sc, axis=-1, keepdims=True)
                expo = jnp.exp(sc - top)
                total = jnp.sum(expo, axis=-1, keepdims=True)
                probs[:, h * TK:(h + 1) * TK] = expo.astype(BF16)
                tops = jnp.where(lane == h, top, tops)
                totals = jnp.where(lane == h, total, totals)
        for n in range(3):
            heads = value_heads[n]
            wide = probs[:, heads[0] * TK:(heads[-1] + 1) * TK]
            wmsg[at, n * 256:(n + 1) * 256] = mm(wide, vm[n]).astype(BF16)
        tops_high, tops_mid = split(tops)
        tops_low = (tops - tops_high.astype(F32) - tops_mid.astype(F32)).astype(BF16)
        totals_high, totals_low = split(totals)
        stats = tops_high.astype(F32)
        for place, piece in enumerate((tops_mid, tops_low, totals_high, totals_low)):
            stats = stats + pltpu.roll(piece.astype(F32), (place + 1) * HEADS, 1)
        wmsg[at, D:MSG] = stats.astype(BF16)

        return chunk

    def far_chunk(step, carry):
        chunk = attend(step)
        for k in range(owners):
            c_copy(chunk * owners + jnp.bitwise_and(c + k, owners - 1)).start()
        return carry

    lax.fori_loop(1, chunks, far_chunk, 0)
    chunk = attend(0)
    for k in range(1, owners):
        c_copy(chunk * owners + jnp.bitwise_and(c + k, owners - 1)).start()
    cbuf[c] = wmsg[own, :]
    mean_high, mean_low = split(mean_own[...])
    hidden_own = mm(mean_high, wagg[...]) + mm(mean_low, wagg[...]) + cond[own, :].astype(F32)
    spread_row = jnp.bitwise_and(iota((256, D), 0), 127)
    spread_col = iota((256, D), 1) - spread_row * HD
    expand[...] = jnp.where(jnp.logical_and(spread_col >= 0, spread_col < HD), 1.0, 0.0).astype(BF16)
    loads["wo"].wait()
    loads["wb"].wait()
    c_all.wait_recv()

    stat = cbuf[:, :, D:MSG].reshape(TQ, 128).astype(F32)
    def piece(k):
        return pltpu.roll(stat, 128 - k * HEADS, 1)

    tops = ((stat + piece(1)) + piece(2)).reshape(NCOL, OWN, 128)
    totals = (piece(3) + piece(4)).reshape(NCOL, OWN, 128)
    best = jnp.max(tops, axis=0, keepdims=True)
    scale = jnp.exp(tops - best)
    total = jnp.sum(scale * totals, axis=0, keepdims=True)
    valid = iota((1, 1, 128), 2) < HEADS
    total = jnp.where(valid, total, 1.0)
    factor = jnp.where(valid, scale / total, 0.0).reshape(TQ, 128)
    factor = jnp.concatenate(split(factor), axis=1)
    attn_parts = []
    for n in range(3):
        cols = slice(n * 256, (n + 1) * 256)
        wide = mm(factor, expand[:, cols])
        terms = cbuf[:, :, cols].astype(F32) * wide.reshape(NCOL, OWN, 256)
        attn_parts.append(jnp.sum(terms, axis=0).astype(BF16))
    attn = jnp.concatenate(attn_parts, axis=1)
    finished = (hidden_own + mm(attn, wo[...])).astype(BF16)

    tokbuf[c] = finished
    d_all = remote(tokbuf.at[others], tokbuf.at[others], dsem, r, next_col)
    def spread_to(peer):
        remote(tokbuf.at[c], tokbuf.at[c], dsem, r, peer).start()

    @pl.when(c != 0)
    def _():
        spread_to(0)

    for k in (8, 7, 6, 5, 4, 3, 2, 1, 15, 14, 13, 12, 11, 10, 9):
        @pl.when(col_at(k) != 0)
        def _():
            spread_to(col_at(k))


    a_all.wait_send()
    b_all.wait_send()

    @pl.when(holds)
    def _():
        for k in range(4):
            cond_copy(held_cond, sibling).wait_send()

    @pl.when(passes_on)
    def _():
        cond_copy(keycond, sibling).wait_send()

    from_sources(keymeans, ksem, lambda copy: copy.wait_send())
    c_all.wait_send()

    d_all.wait_recv()
    token_store = pltpu.make_async_copy(tokbuf, token_out_h, osem.at[0])
    token_store.start()
    chosen = mm(pick[...], tokbuf[...].reshape(TQ, D)).astype(BF16)
    atomv[...] = (feats[...].astype(F32) + mm(chosen, wb[...])).astype(BF16)
    atom_store = pltpu.make_async_copy(atomv, atom_out_h, osem.at[1])
    atom_store.start()
    d_all.wait_send()
    token_store.wait()
    atom_store.wait()


def hand_over(token_in, atom_in, token_out, atom_out, sems):
    copies = [
        pltpu.make_async_copy(token_in, token_out, sems.at[0]),
        pltpu.make_async_copy(atom_in, atom_out, sems.at[1]),
    ]
    for copy in copies:
        copy.start()
    for copy in copies:
        copy.wait()


def local(
    atom_feats, atom_token, atom_counts, token_cond, pair, token_gain, pair_gain, w_bias, w_agg, w_query, w_keyval,
    w_out, w_back,
):
    any_space = pl.BlockSpec(memory_space=pl.ANY)
    hbm = pl.BlockSpec(memory_space=pltpu.HBM)
    vmem = pltpu.VMEM
    dma = pltpu.SemaphoreType.DMA
    scratch = [
        vmem((CA, CA), BF16), vmem((1, CA), jnp.int32), vmem((1, TQ), jnp.int32), vmem((TQ, D), BF16),
        vmem((TQ, TK, CA), BF16), vmem((6, 128), F32), vmem((1, CA), F32), vmem((HEADS, CA), BF16),
        vmem((CA, D), BF16), vmem((D, D), BF16), vmem((D, 2 * D), BF16), vmem((D, D), BF16), vmem((D, CA), BF16),
        vmem((3 * HEADS, 2 * CA), BF16), vmem((HEADS, CA), F32), vmem((HEADS * TQ, TK), F32), vmem((TQ, TK), F32),
        vmem((TQ, TK), F32), vmem((TQ, CA), BF16), vmem((NCOL, OWN, CA), BF16), vmem((TQ, CA), BF16), vmem((OWN, CA), F32),
        vmem((TQ, CA), F32),
        vmem((TQ, D), F32), vmem((TQ, D), BF16), vmem((TQ, D), BF16), vmem((TK, 2 * D), BF16),
        vmem((8, OWN, CA), BF16), vmem((TK, D), BF16),
        vmem((HEADS // 2, 2 * TK, 256), BF16), vmem((3, 6 * TK, 256), BF16), vmem((CHUNK, HEADS * TK), BF16),
        vmem((TQ, MSG), BF16), vmem((NCOL, OWN, MSG), BF16), vmem((256, D), BF16), vmem((NCOL, OWN, D), BF16),
        vmem((CA, TQ), BF16), vmem((CA, CA), BF16),
        dma((13,)), dma((PAIR_PARTS,)), dma((2,)),
        *[dma((2,))] * 6,
    ]
    outs = pl.pallas_call(
        kernel,
        out_shape=(jax.ShapeDtypeStruct((NCOL, OWN, D), BF16), jax.ShapeDtypeStruct((CA, CA), BF16)),
        in_specs=[hbm] * 13,
        out_specs=(any_space, any_space),
        scratch_shapes=scratch,
        compiler_params=pltpu.CompilerParams(
            collective_id=0, has_side_effects=True, vmem_limit_bytes=40 * 1024 * 1024),
        name="diffusion_block",
    )(*[pltpu.with_memory_space_constraint(x, pltpu.HBM) for x in (
        atom_feats, atom_token.reshape(1, CA), atom_counts.reshape(1, TQ), token_cond, pair, token_gain.reshape(6, 128),
        pair_gain.reshape(1, CA), w_bias.T, w_agg, w_query, w_keyval, w_out, w_back,
    )])
    stored = pl.pallas_call(
        hand_over,
        out_shape=(jax.ShapeDtypeStruct((NCOL, OWN, D), BF16), jax.ShapeDtypeStruct((CA, CA), BF16)),
        in_specs=[any_space] * 2,
        out_specs=(any_space, any_space),
        scratch_shapes=[dma((2,))],
        compiler_params=pltpu.CompilerParams(vmem_limit_bytes=1024 * 1024),
        name="hand_over",
    )(*outs)
    return stored[0].reshape(TQ, D), stored[1]


def solution(mesh):
    placed = (
        P(("row", "col"), None), P(("row", "col")), P("row"), P("row", None), P("row", "col", None),
        P(), P(), P(), P(), P(), P(), P(), P(),
    )
    return jax.shard_map(
        local,
        mesh=mesh,
        in_specs=placed,
        out_specs=(P("row", None), P(("row", "col"), None)),
        check_vma=False,
    )
```

```python
import math

import jax
import jax.numpy as jnp
from jax import lax
from jax.experimental import pallas as pl
from jax.experimental.pallas import tpu as pltpu
from jax.sharding import PartitionSpec as P

D = 768
HEADS = 16
HD = 48
CA = 128
TQ = 256
TK = 128
NCOL = 16
NROW = 8
OWN = TQ // NCOL
MSG = D + 128
CHUNK = 128
PAIR_PARTS = 8
PART_ROWS = TQ // PAIR_PARTS
FIRST_PARTS = 4
PASS_PART = 6
MESH = pl.DeviceIdType.MESH
F32 = jnp.float32
BF16 = jnp.bfloat16


def mm(a, b):
    return jnp.dot(a, b, preferred_element_type=F32)


def mm_nt(a, b):
    return lax.dot_general(a, b, (((1,), (1,)), ((), ())), preferred_element_type=F32)


def iota(shape, axis):
    return lax.broadcasted_iota(jnp.int32, shape, axis)


def split(x):
    high = x.astype(BF16)
    low = (x - high.astype(F32)).astype(BF16)
    return high, low


def rows_of(index, size):
    return pl.ds(pl.multiple_of(index * size, size), size)


def kernel(
    feats_h, tok_h, counts_h, cond_h, pair_h, tgain_h, pgain_h, wbias_h, wagg_h, wq_h, wkv_h, wo_h, wb_h,
    token_out_h, atom_out_h,
    feats, tok, counts, cond, pair, tgain, pgain, wbias, wagg, wq, wkv, wo, wb,
    gmat, colsum, bias, s1, s2, part, abuf, means, mean_own, cnt, aggv, normed, qv, kv, keymeans, keycond,
    km, vm, probs, wmsg, cbuf, expand, tokbuf, pick, atomv,
    lsem, psem, osem, asem, bsem, ksem, csem, qsem, dsem,
):
    r = lax.axis_index("row")
    c = lax.axis_index("col")
    key_col = 2 * r + lax.shift_right_logical(c, 3)
    key_slot = jnp.bitwise_and(c, 7)
    src_row = lax.shift_right_logical(c, 1)
    src_col = 8 * jnp.bitwise_and(c, 1)
    is_self = c == key_col
    other = jnp.logical_not(is_self)
    holds = r == src_row
    same_core = jnp.bitwise_and(r, 1) == jnp.bitwise_and(src_row, 1)
    sibling = jnp.bitwise_xor(r, 1)
    passes_on = jnp.logical_and(same_core, jnp.logical_not(holds))

    def col_at(offset):
        return jnp.bitwise_and(c + offset, NCOL - 1)

    next_col = col_at(1)
    turn = 1 - 2 * jnp.bitwise_and(r, 1)

    def local(i, src, dst):
        return pltpu.make_async_copy(src, dst, lsem.at[i])

    loads = {
        "feats": local(0, feats_h, feats),
        "tok": local(1, tok_h, tok),
        "counts": local(2, counts_h, counts),
        "wbias": local(3, wbias_h, wbias),
        "pgain": local(4, pgain_h, pgain),
        "wagg": local(5, wagg_h, wagg),
        "cond": local(7, cond_h, cond),
        "tgain": local(8, tgain_h, tgain),
        "wq": local(9, wq_h, wq),
        "wkv": local(10, wkv_h, wkv),
        "wo": local(11, wo_h, wo),
        "wb": local(12, wb_h, wb),
    }

    def pair_load(k):
        at = pl.ds(k * PART_ROWS, PART_ROWS)
        return pltpu.make_async_copy(pair_h.at[at], pair.at[at], psem.at[k])

    for name in ("feats", "tok", "counts", "wbias", "pgain"):
        loads[name].start()

    barrier = pltpu.get_barrier_semaphore()

    def greet(row, col):
        pl.semaphore_signal(barrier, inc=1, device_id=(row, col), device_id_type=MESH)

    for k in range(1, NCOL):
        greet(r, col_at(k))
    for k in range(1, 8):
        greet(src_row, src_col + jnp.bitwise_and(c + k, 7))

    @pl.when(other)
    def _():
        greet(src_row, src_col + key_slot)

    @pl.when(jnp.logical_not(holds))
    def _():
        greet(jnp.where(same_core, src_row, sibling), c)

    for k in range(3):
        pair_load(k).start()

    loads["feats"].wait()
    loads["tok"].wait()
    here = tok[...] - r * TQ
    member = jnp.where(iota((TQ, CA), 0) == here, 1.0, 0.0).astype(BF16)
    part[...] = mm(member, feats[...]).astype(BF16)

    pl.semaphore_wait(
        barrier,
        NCOL - 1 + 8 - is_self.astype(jnp.int32) + 4 * holds.astype(jnp.int32) + passes_on.astype(jnp.int32))

    def remote(src, dst, sems, row, col):
        return pltpu.make_async_remote_copy(
            src_ref=src, dst_ref=dst, send_sem=sems.at[0], recv_sem=sems.at[1],
            device_id=(row, col), device_id_type=MESH)

    others = pl.ds(0, NCOL - 1)
    other_rows = pl.ds(0, (NCOL - 1) * OWN)

    def a_copy(peer):
        return remote(part.at[rows_of(peer, OWN)], abuf.at[c], asem, r, peer)

    a_all = remote(part.at[other_rows], abuf.at[others], asem, r, next_col)

    def each_peer(action):
        for k in (8, 9, 10, 11, 12, 13, 14, 15, 1, 2, 3, 4, 5, 6, 7):
            action(col_at(turn * k))

    each_peer(lambda peer: a_copy(peer).start())
    for name in ("wagg", "cond", "tgain"):
        loads[name].start()
    for k in range(3, PAIR_PARTS):
        pair_load(k).start()
    for name in ("wq", "wkv", "wo", "wb"):
        loads[name].start()

    def each_target(action):
        for k in range(1, NROW):
            action(jnp.bitwise_and(r + k, NROW - 1))

        @pl.when(other)
        def _():
            action(r)

    def from_sources(buffer, sems, action):
        for count in (7, 8):
            @pl.when(is_self == (count == 7))
            def _():
                action(remote(buffer.at[pl.ds(0, count)], buffer.at[pl.ds(0, count)], sems, r, next_col))

    held_cond = cond_h.at[rows_of(jnp.bitwise_and(c, 1), TK)]

    def cond_copy(source, row):
        return remote(source, keycond, qsem, row, c)

    @pl.when(holds)
    def _():
        for k in (4, 2, 6):
            cond_copy(held_cond, jnp.bitwise_and(r + k, NROW - 1)).start()
        cond_copy(held_cond, sibling).start()

    abuf[c] = part[rows_of(c, OWN), :]

    eye = iota((CA, CA), 0) == iota((CA, CA), 1)
    eye_b = jnp.where(eye, 1.0, 0.0).astype(BF16)
    pick[...] = mm_nt(eye_b, member).astype(BF16)
    loads["wbias"].wait()
    loads["pgain"].wait()
    gain_t = (wbias[...].astype(F32) * pgain[...]).astype(BF16)
    none = jnp.zeros((HEADS, CA), BF16)
    place = iota((HEADS, CA), 0)
    ones_left = jnp.where(place == 0, 1.0, 0.0).astype(BF16)
    ones_right = jnp.where(place == 1, 1.0, 0.0).astype(BF16)
    gmat[:, 0:CA] = jnp.concatenate([gain_t, none, ones_left], axis=0)
    gmat[:, CA:2 * CA] = jnp.concatenate([none, gain_t, ones_right], axis=0)
    colsum[...] = jnp.broadcast_to(jnp.sum(gain_t.astype(F32), axis=1, keepdims=True), (HEADS, CA))
    loads["counts"].wait()
    for half in range(2):
        line = counts[:, half * CA:(half + 1) * CA].astype(F32)
        column = jnp.sum(jnp.where(eye, jnp.broadcast_to(line, (CA, CA)), 0.0), axis=1, keepdims=True)
        cnt[half * CA:(half + 1) * CA, :] = jnp.broadcast_to(column, (CA, CA))

    def bias_rows(k):
        pair_load(k).wait()

        def four(j, carry):
            first = k * PART_ROWS + 4 * j
            blocks = [jnp.transpose(pair[first + e]) for e in range(4)]
            for e in range(4):
                wide = blocks[e].astype(F32)
                s2[pl.ds(first + e, 1), :] = jnp.sum(wide * wide, axis=0, keepdims=True)
            square = jnp.concatenate(
                [jnp.concatenate(blocks[0:2], axis=1), jnp.concatenate(blocks[2:4], axis=1)], axis=0)
            sums = mm(gmat[...], square)
            for e in range(4):
                low, side = e // 2, slice((e % 2) * CA, (e % 2 + 1) * CA)
                bias[pl.ds(first + e, HEADS, stride=TQ), :] = sums[low * HEADS:(low + 1) * HEADS, side]
                s1[pl.ds(first + e, 1), :] = sums[2 * HEADS + low:2 * HEADS + low + 1, side]
            return carry

        lax.fori_loop(0, PART_ROWS // 4, four, 0, unroll=8)

    for k in range(FIRST_PARTS):
        bias_rows(k)

    a_all.wait_recv()
    own = rows_of(c, OWN)
    mean_own[...] = jnp.sum(abuf[...].astype(F32), axis=0) / cnt[own, :]
    means[own, :] = mean_own[...].astype(BF16)

    def k_copy(target):
        return remote(means.at[own], keymeans.at[key_slot], ksem, target, key_col)

    def b_copy(peer):
        return remote(means.at[own], means.at[own], bsem, r, peer)

    b_all = remote(means.at[other_rows], means.at[other_rows], bsem, r, next_col)
    each_target(lambda target: k_copy(target).start())
    each_peer(lambda peer: b_copy(peer).start())

    @pl.when(is_self)
    def _():
        keymeans[key_slot] = means[own, :]

    for k in range(FIRST_PARTS, PASS_PART):
        bias_rows(k)

    @pl.when(passes_on)
    def _():
        arrived = cond_copy(keycond, sibling)
        arrived.wait_recv()
        arrived.start()

    for k in range(PASS_PART, PAIR_PARTS):
        bias_rows(k)

    def normalize(hidden):
        center = hidden - jnp.mean(hidden, axis=-1, keepdims=True)
        spread = jnp.mean(center * center, axis=-1, keepdims=True)
        gain = jnp.concatenate([tgain[k:k + 1, :] for k in range(6)], axis=1)
        return (center * lax.rsqrt(spread + 1e-05) * gain).astype(BF16)

    for name in ("wagg", "cond", "tgain", "wq", "wkv"):
        loads[name].wait()
    @pl.when(holds)
    def _():
        keycond[...] = cond[rows_of(jnp.bitwise_and(c, 1), TK), :]

    @pl.when(jnp.logical_not(same_core))
    def _():
        cond_copy(keycond, sibling).wait_recv()

    from_sources(keymeans, ksem, lambda copy: copy.wait_recv())
    b_all.wait_recv()
    key_agg = mm(keymeans[...].reshape(TK, CA), wagg[...])
    aggv[...] = mm(means[...], wagg[...])
    key_rows = normalize(key_agg + keycond[...].astype(F32))
    for n in range(6):
        cols = slice(n * 256, (n + 1) * 256)
        kv[:, cols] = mm(key_rows, wkv[:, cols]).astype(BF16)
    for k in range(TQ // 64):
        at = slice(k * 64, (k + 1) * 64)
        normed[at, :] = normalize(aggv[at, :] + cond[at, :].astype(F32))
    for n in range(3):
        cols = slice(n * 256, (n + 1) * 256)
        qv[:, cols] = (mm(normed[...], wq[:, cols]) * (1.0 / math.sqrt(HD))).astype(BF16)

    def head_mask(first, width, head):
        lane = iota((1, width), 1) + first
        return jnp.where(jnp.logical_and(lane >= head * HD, lane < (head + 1) * HD), 1.0, 0.0).astype(BF16)

    windows = []
    for p in range(HEADS // 2):
        first = (2 * p * HD) // 128 * 128
        last = -(-((2 * p + 2) * HD) // 128) * 128
        windows.append((first, last - first))
        block = kv[:, first:last]
        for e in range(2):
            km[p, e * TK:(e + 1) * TK, 0:last - first] = block * head_mask(first, last - first, 2 * p + e)
    value_heads = []
    for n in range(3):
        heads = [h for h in range(HEADS) if h * HD < (n + 1) * 256 and (h + 1) * HD > n * 256]
        value_heads.append(heads)
        block = kv[:, D + n * 256:D + (n + 1) * 256]
        for slot, h in enumerate(heads):
            vm[n, slot * TK:(slot + 1) * TK, :] = block * head_mask(n * 256, 256, h)

    def c_copy(owner):
        return remote(wmsg.at[rows_of(owner, OWN)], cbuf.at[c], csem, r, owner)

    c_all = remote(wmsg.at[other_rows], cbuf.at[others], csem, r, next_col)
    owners = CHUNK // OWN
    chunks = TQ // CHUNK

    def attend(step):
        chunk = jnp.bitwise_and(lax.shift_right_logical(c, 3) + step, chunks - 1)
        at = rows_of(chunk, CHUNK)
        mean = s1[at, :] * (1.0 / CA)
        mean_high, mean_low = split(mean)
        mean_high = mean_high.astype(F32)
        mean_low = mean - mean_high
        var = (s2[at, :] * (1.0 / CA) - mean_high * mean_high) - mean_low * (mean_high + mean)
        rstd = lax.rsqrt(jnp.maximum(var, 0.0) + 1e-05)
        lane = iota((CHUNK, 128), 1)
        tops = jnp.zeros((CHUNK, 128), F32)
        totals = jnp.zeros((CHUNK, 128), F32)
        for p in range(HEADS // 2):
            first, width = windows[p]
            scores = mm_nt(qv[at, first:first + width], km[p, :, 0:width])
            for e in range(2):
                h = 2 * p + e
                raw = bias[pl.ds(pl.multiple_of(h * TQ + chunk * CHUNK, CHUNK), CHUNK), :]
                sc = scores[:, e * TK:(e + 1) * TK] + (raw - mean * colsum[h:h + 1, :]) * rstd
                top = jnp.max(sc, axis=-1, keepdims=True)
                expo = jnp.exp(sc - top)
                total = jnp.sum(expo, axis=-1, keepdims=True)
                probs[:, h * TK:(h + 1) * TK] = expo.astype(BF16)
                tops = jnp.where(lane == h, top, tops)
                totals = jnp.where(lane == h, total, totals)
        for n in range(3):
            heads = value_heads[n]
            wide = probs[:, heads[0] * TK:(heads[-1] + 1) * TK]
            wmsg[at, n * 256:(n + 1) * 256] = mm(wide, vm[n]).astype(BF16)
        tops_high, tops_mid = split(tops)
        tops_low = (tops - tops_high.astype(F32) - tops_mid.astype(F32)).astype(BF16)
        totals_high, totals_low = split(totals)
        stats = tops_high.astype(F32)
        for place, piece in enumerate((tops_mid, tops_low, totals_high, totals_low)):
            stats = stats + pltpu.roll(piece.astype(F32), (place + 1) * HEADS, 1)
        wmsg[at, D:MSG] = stats.astype(BF16)

        return chunk

    def far_chunk(step, carry):
        chunk = attend(step)
        for k in range(owners):
            c_copy(chunk * owners + jnp.bitwise_and(c + turn * k, owners - 1)).start()
        return carry

    lax.fori_loop(1, chunks, far_chunk, 0)
    chunk = attend(0)
    for k in range(1, owners):
        c_copy(chunk * owners + jnp.bitwise_and(c + turn * k, owners - 1)).start()
    cbuf[c] = wmsg[own, :]
    mean_high, mean_low = split(mean_own[...])
    hidden_own = mm(mean_high, wagg[...]) + mm(mean_low, wagg[...]) + cond[own, :].astype(F32)
    spread_row = jnp.bitwise_and(iota((256, D), 0), 127)
    spread_col = iota((256, D), 1) - spread_row * HD
    expand[...] = jnp.where(jnp.logical_and(spread_col >= 0, spread_col < HD), 1.0, 0.0).astype(BF16)
    loads["wo"].wait()
    loads["wb"].wait()
    c_all.wait_recv()

    stat = cbuf[:, :, D:MSG].reshape(TQ, 128).astype(F32)
    def piece(k):
        return pltpu.roll(stat, 128 - k * HEADS, 1)

    tops = ((stat + piece(1)) + piece(2)).reshape(NCOL, OWN, 128)
    totals = (piece(3) + piece(4)).reshape(NCOL, OWN, 128)
    best = jnp.max(tops, axis=0, keepdims=True)
    scale = jnp.exp(tops - best)
    total = jnp.sum(scale * totals, axis=0, keepdims=True)
    valid = iota((1, 1, 128), 2) < HEADS
    total = jnp.where(valid, total, 1.0)
    factor = jnp.where(valid, scale / total, 0.0).reshape(TQ, 128)
    factor = jnp.concatenate(split(factor), axis=1)
    attn_parts = []
    for n in range(3):
        cols = slice(n * 256, (n + 1) * 256)
        wide = mm(factor, expand[:, cols])
        terms = cbuf[:, :, cols].astype(F32) * wide.reshape(NCOL, OWN, 256)
        attn_parts.append(jnp.sum(terms, axis=0).astype(BF16))
    attn = jnp.concatenate(attn_parts, axis=1)
    finished = (hidden_own + mm(attn, wo[...])).astype(BF16)

    tokbuf[c] = finished
    d_all = remote(tokbuf.at[others], tokbuf.at[others], dsem, r, next_col)
    def spread_to(peer):
        remote(tokbuf.at[c], tokbuf.at[c], dsem, r, peer).start()

    @pl.when(c != 0)
    def _():
        spread_to(0)

    for k in (8, 7, 6, 5, 4, 3, 2, 1, 15, 14, 13, 12, 11, 10, 9):
        @pl.when(col_at(turn * k) != 0)
        def _():
            spread_to(col_at(turn * k))


    a_all.wait_send()
    b_all.wait_send()

    @pl.when(holds)
    def _():
        for k in range(4):
            cond_copy(held_cond, sibling).wait_send()

    @pl.when(passes_on)
    def _():
        cond_copy(keycond, sibling).wait_send()

    from_sources(keymeans, ksem, lambda copy: copy.wait_send())
    c_all.wait_send()

    d_all.wait_recv()
    token_store = pltpu.make_async_copy(tokbuf, token_out_h, osem.at[0])
    token_store.start()
    chosen = mm(pick[...], tokbuf[...].reshape(TQ, D)).astype(BF16)
    atomv[...] = (feats[...].astype(F32) + mm(chosen, wb[...])).astype(BF16)
    atom_store = pltpu.make_async_copy(atomv, atom_out_h, osem.at[1])
    atom_store.start()
    d_all.wait_send()
    token_store.wait()
    atom_store.wait()


def hand_over(token_in, atom_in, token_out, atom_out, sems):
    copies = [
        pltpu.make_async_copy(token_in, token_out, sems.at[0]),
        pltpu.make_async_copy(atom_in, atom_out, sems.at[1]),
    ]
    for copy in copies:
        copy.start()
    for copy in copies:
        copy.wait()


def local(
    atom_feats, atom_token, atom_counts, token_cond, pair, token_gain, pair_gain, w_bias, w_agg, w_query, w_keyval,
    w_out, w_back,
):
    any_space = pl.BlockSpec(memory_space=pl.ANY)
    hbm = pl.BlockSpec(memory_space=pltpu.HBM)
    vmem = pltpu.VMEM
    dma = pltpu.SemaphoreType.DMA
    scratch = [
        vmem((CA, CA), BF16), vmem((1, CA), jnp.int32), vmem((1, TQ), jnp.int32), vmem((TQ, D), BF16),
        vmem((TQ, TK, CA), BF16), vmem((6, 128), F32), vmem((1, CA), F32), vmem((HEADS, CA), BF16),
        vmem((CA, D), BF16), vmem((D, D), BF16), vmem((D, 2 * D), BF16), vmem((D, D), BF16), vmem((D, CA), BF16),
        vmem((3 * HEADS, 2 * CA), BF16), vmem((HEADS, CA), F32), vmem((HEADS * TQ, TK), F32), vmem((TQ, TK), F32),
        vmem((TQ, TK), F32), vmem((TQ, CA), BF16), vmem((NCOL, OWN, CA), BF16), vmem((TQ, CA), BF16), vmem((OWN, CA), F32),
        vmem((TQ, CA), F32),
        vmem((TQ, D), F32), vmem((TQ, D), BF16), vmem((TQ, D), BF16), vmem((TK, 2 * D), BF16),
        vmem((8, OWN, CA), BF16), vmem((TK, D), BF16),
        vmem((HEADS // 2, 2 * TK, 256), BF16), vmem((3, 6 * TK, 256), BF16), vmem((CHUNK, HEADS * TK), BF16),
        vmem((TQ, MSG), BF16), vmem((NCOL, OWN, MSG), BF16), vmem((256, D), BF16), vmem((NCOL, OWN, D), BF16),
        vmem((CA, TQ), BF16), vmem((CA, CA), BF16),
        dma((13,)), dma((PAIR_PARTS,)), dma((2,)),
        *[dma((2,))] * 6,
    ]
    outs = pl.pallas_call(
        kernel,
        out_shape=(jax.ShapeDtypeStruct((NCOL, OWN, D), BF16), jax.ShapeDtypeStruct((CA, CA), BF16)),
        in_specs=[hbm] * 13,
        out_specs=(any_space, any_space),
        scratch_shapes=scratch,
        compiler_params=pltpu.CompilerParams(
            collective_id=0, has_side_effects=True, vmem_limit_bytes=40 * 1024 * 1024),
        name="diffusion_block",
    )(*[pltpu.with_memory_space_constraint(x, pltpu.HBM) for x in (
        atom_feats, atom_token.reshape(1, CA), atom_counts.reshape(1, TQ), token_cond, pair, token_gain.reshape(6, 128),
        pair_gain.reshape(1, CA), w_bias.T, w_agg, w_query, w_keyval, w_out, w_back,
    )])
    stored = pl.pallas_call(
        hand_over,
        out_shape=(jax.ShapeDtypeStruct((NCOL, OWN, D), BF16), jax.ShapeDtypeStruct((CA, CA), BF16)),
        in_specs=[any_space] * 2,
        out_specs=(any_space, any_space),
        scratch_shapes=[dma((2,))],
        compiler_params=pltpu.CompilerParams(vmem_limit_bytes=1024 * 1024),
        name="hand_over",
    )(*outs)
    return stored[0].reshape(TQ, D), stored[1]


def solution(mesh):
    placed = (
        P(("row", "col"), None), P(("row", "col")), P("row"), P("row", None), P("row", "col", None),
        P(), P(), P(), P(), P(), P(), P(), P(),
    )
    return jax.shard_map(
        local,
        mesh=mesh,
        in_specs=placed,
        out_specs=(P("row", None), P(("row", "col"), None)),
        check_vma=False,
    )
```

```python
import math

import jax
import jax.numpy as jnp
from jax import lax
from jax.experimental import pallas as pl
from jax.experimental.pallas import tpu as pltpu
from jax.sharding import PartitionSpec as P

D = 768
HEADS = 16
HD = 48
CA = 128
TQ = 256
TK = 128
NCOL = 16
NROW = 8
OWN = TQ // NCOL
MSG = D + 128
CHUNK = 128
PAIR_PARTS = 8
PART_ROWS = TQ // PAIR_PARTS
FIRST_PARTS = 4
PASS_PART = 6
MESH = pl.DeviceIdType.MESH
F32 = jnp.float32
BF16 = jnp.bfloat16


def mm(a, b):
    return jnp.dot(a, b, preferred_element_type=F32)


def mm_nt(a, b):
    return lax.dot_general(a, b, (((1,), (1,)), ((), ())), preferred_element_type=F32)


def iota(shape, axis):
    return lax.broadcasted_iota(jnp.int32, shape, axis)


def split(x):
    high = x.astype(BF16)
    low = (x - high.astype(F32)).astype(BF16)
    return high, low


def rows_of(index, size):
    return pl.ds(pl.multiple_of(index * size, size), size)


def kernel(
    feats_h, tok_h, counts_h, cond_h, pair_h, tgain_h, pgain_h, wbias_h, wagg_h, wq_h, wkv_h, wo_h, wb_h,
    token_out_h, atom_out_h,
    feats, tok, counts, cond, pair, tgain, pgain, wbias, wagg, wq, wkv, wo, wb,
    gmat, colsum, bias, s1, s2, part, abuf, means, mean_own, cnt, aggv, normed, qv, kv, keymeans, keycond,
    km, vm, probs, wmsg, cbuf, expand, tokbuf, pick, atomv,
    lsem, psem, osem, asem, bsem, ksem, csem, qsem, dsem,
):
    r = lax.axis_index("row")
    c = lax.axis_index("col")
    key_col = 2 * r + lax.shift_right_logical(c, 3)
    key_slot = jnp.bitwise_and(c, 7)
    src_row = lax.shift_right_logical(c, 1)
    src_col = 8 * jnp.bitwise_and(c, 1)
    is_self = c == key_col
    other = jnp.logical_not(is_self)
    holds = r == src_row
    same_core = jnp.bitwise_and(r, 1) == jnp.bitwise_and(src_row, 1)
    sibling = jnp.bitwise_xor(r, 1)
    passes_on = jnp.logical_and(same_core, jnp.logical_not(holds))

    def col_at(offset):
        return jnp.bitwise_and(c + offset, NCOL - 1)

    next_col = col_at(1)
    turn = 1 - 2 * jnp.bitwise_and(r, 1)

    def local(i, src, dst):
        return pltpu.make_async_copy(src, dst, lsem.at[i])

    loads = {
        "feats": local(0, feats_h, feats),
        "tok": local(1, tok_h, tok),
        "counts": local(2, counts_h, counts),
        "wbias": local(3, wbias_h, wbias),
        "pgain": local(4, pgain_h, pgain),
        "wagg": local(5, wagg_h, wagg),
        "cond": local(7, cond_h, cond),
        "tgain": local(8, tgain_h, tgain),
        "wq": local(9, wq_h, wq),
        "wkv": local(10, wkv_h, wkv),
        "wo": local(11, wo_h, wo),
        "wb": local(12, wb_h, wb),
    }

    def pair_load(k):
        at = pl.ds(k * PART_ROWS, PART_ROWS)
        return pltpu.make_async_copy(pair_h.at[at], pair.at[at], psem.at[k])

    for name in ("feats", "tok", "counts", "wbias", "pgain"):
        loads[name].start()

    barrier = pltpu.get_barrier_semaphore()

    def greet(row, col):
        pl.semaphore_signal(barrier, inc=1, device_id=(row, col), device_id_type=MESH)

    for k in range(1, NCOL):
        greet(r, col_at(k))
    for k in range(1, 8):
        greet(src_row, src_col + jnp.bitwise_and(c + k, 7))

    @pl.when(other)
    def _():
        greet(src_row, src_col + key_slot)

    @pl.when(jnp.logical_not(holds))
    def _():
        greet(jnp.where(same_core, src_row, sibling), c)

    for k in range(3):
        pair_load(k).start()

    loads["feats"].wait()
    loads["tok"].wait()
    here = tok[...] - r * TQ
    member = jnp.where(iota((TQ, CA), 0) == here, 1.0, 0.0).astype(BF16)
    part[...] = mm(member, feats[...]).astype(BF16)

    pl.semaphore_wait(
        barrier,
        NCOL - 1 + 8 - is_self.astype(jnp.int32) + 4 * holds.astype(jnp.int32) + passes_on.astype(jnp.int32))

    def remote(src, dst, sems, row, col):
        return pltpu.make_async_remote_copy(
            src_ref=src, dst_ref=dst, send_sem=sems.at[0], recv_sem=sems.at[1],
            device_id=(row, col), device_id_type=MESH)

    others = pl.ds(0, NCOL - 1)
    other_rows = pl.ds(0, (NCOL - 1) * OWN)

    def a_copy(peer):
        return remote(part.at[rows_of(peer, OWN)], abuf.at[c], asem, r, peer)

    a_all = remote(part.at[other_rows], abuf.at[others], asem, r, next_col)

    def each_peer(action):
        for k in (8, 9, 10, 11, 12, 13, 14, 15, 1, 2, 3, 4, 5, 6, 7):
            action(col_at(turn * k))

    each_peer(lambda peer: a_copy(peer).start())
    for name in ("wagg", "cond", "tgain"):
        loads[name].start()
    for k in range(3, PAIR_PARTS):
        pair_load(k).start()
    for name in ("wq", "wkv", "wo", "wb"):
        loads[name].start()

    def each_target(action):
        for k in range(1, NROW):
            action(jnp.bitwise_and(r + k, NROW - 1))

        @pl.when(other)
        def _():
            action(r)

    def from_sources(buffer, sems, action):
        for count in (7, 8):
            @pl.when(is_self == (count == 7))
            def _():
                action(remote(buffer.at[pl.ds(0, count)], buffer.at[pl.ds(0, count)], sems, r, next_col))

    held_cond = cond_h.at[rows_of(jnp.bitwise_and(c, 1), TK)]

    def cond_copy(source, row):
        return remote(source, keycond, qsem, row, c)

    @pl.when(holds)
    def _():
        for k in (4, 2, 6):
            cond_copy(held_cond, jnp.bitwise_and(r + k, NROW - 1)).start()
        cond_copy(held_cond, sibling).start()

    abuf[c] = part[rows_of(c, OWN), :]

    eye = iota((CA, CA), 0) == iota((CA, CA), 1)
    eye_b = jnp.where(eye, 1.0, 0.0).astype(BF16)
    pick[...] = mm_nt(eye_b, member).astype(BF16)
    loads["wbias"].wait()
    loads["pgain"].wait()
    gain_t = (wbias[...].astype(F32) * pgain[...]).astype(BF16)
    none = jnp.zeros((HEADS, CA), BF16)
    place = iota((HEADS, CA), 0)
    ones_left = jnp.where(place == 0, 1.0, 0.0).astype(BF16)
    ones_right = jnp.where(place == 1, 1.0, 0.0).astype(BF16)
    gmat[:, 0:CA] = jnp.concatenate([gain_t, none, ones_left], axis=0)
    gmat[:, CA:2 * CA] = jnp.concatenate([none, gain_t, ones_right], axis=0)
    colsum[...] = jnp.broadcast_to(jnp.sum(gain_t.astype(F32), axis=1, keepdims=True), (HEADS, CA))
    loads["counts"].wait()
    for half in range(2):
        line = counts[:, half * CA:(half + 1) * CA].astype(F32)
        column = jnp.sum(jnp.where(eye, jnp.broadcast_to(line, (CA, CA)), 0.0), axis=1, keepdims=True)
        cnt[half * CA:(half + 1) * CA, :] = jnp.broadcast_to(column, (CA, CA))

    def bias_rows(k):
        pair_load(k).wait()

        def four(j, carry):
            first = k * PART_ROWS + 4 * j
            blocks = [jnp.transpose(pair[first + e]) for e in range(4)]
            for e in range(4):
                wide = blocks[e].astype(F32)
                s2[pl.ds(first + e, 1), :] = jnp.sum(wide * wide, axis=0, keepdims=True)
            square = jnp.concatenate(
                [jnp.concatenate(blocks[0:2], axis=1), jnp.concatenate(blocks[2:4], axis=1)], axis=0)
            sums = mm(gmat[...], square)
            for e in range(4):
                low, side = e // 2, slice((e % 2) * CA, (e % 2 + 1) * CA)
                bias[pl.ds(first + e, HEADS, stride=TQ), :] = sums[low * HEADS:(low + 1) * HEADS, side]
                s1[pl.ds(first + e, 1), :] = sums[2 * HEADS + low:2 * HEADS + low + 1, side]
            return carry

        lax.fori_loop(0, PART_ROWS // 4, four, 0, unroll=8)

    for k in range(FIRST_PARTS):
        bias_rows(k)

    a_all.wait_recv()
    own = rows_of(c, OWN)
    mean_own[...] = jnp.sum(abuf[...].astype(F32), axis=0) / cnt[own, :]
    means[own, :] = mean_own[...].astype(BF16)

    def k_copy(target):
        return remote(means.at[own], keymeans.at[key_slot], ksem, target, key_col)

    def b_copy(peer):
        return remote(means.at[own], means.at[own], bsem, r, peer)

    b_all = remote(means.at[other_rows], means.at[other_rows], bsem, r, next_col)
    each_target(lambda target: k_copy(target).start())
    each_peer(lambda peer: b_copy(peer).start())

    @pl.when(is_self)
    def _():
        keymeans[key_slot] = means[own, :]

    for k in range(FIRST_PARTS, PASS_PART):
        bias_rows(k)

    @pl.when(passes_on)
    def _():
        arrived = cond_copy(keycond, sibling)
        arrived.wait_recv()
        arrived.start()

    for k in range(PASS_PART, PAIR_PARTS):
        bias_rows(k)

    def normalize(hidden):
        center = hidden - jnp.mean(hidden, axis=-1, keepdims=True)
        spread = jnp.mean(center * center, axis=-1, keepdims=True)
        gain = jnp.concatenate([tgain[k:k + 1, :] for k in range(6)], axis=1)
        return (center * lax.rsqrt(spread + 1e-05) * gain).astype(BF16)

    for name in ("wagg", "cond", "tgain", "wq", "wkv"):
        loads[name].wait()
    @pl.when(holds)
    def _():
        keycond[...] = cond[rows_of(jnp.bitwise_and(c, 1), TK), :]

    @pl.when(jnp.logical_not(same_core))
    def _():
        cond_copy(keycond, sibling).wait_recv()

    from_sources(keymeans, ksem, lambda copy: copy.wait_recv())
    b_all.wait_recv()
    key_agg = mm(keymeans[...].reshape(TK, CA), wagg[...])
    aggv[...] = mm(means[...], wagg[...])
    key_rows = normalize(key_agg + keycond[...].astype(F32))
    for n in range(6):
        cols = slice(n * 256, (n + 1) * 256)
        kv[:, cols] = mm(key_rows, wkv[:, cols]).astype(BF16)
    for k in range(TQ // 64):
        at = slice(k * 64, (k + 1) * 64)
        normed[at, :] = normalize(aggv[at, :] + cond[at, :].astype(F32))
    for n in range(3):
        cols = slice(n * 256, (n + 1) * 256)
        qv[:, cols] = (mm(normed[...], wq[:, cols]) * (1.0 / math.sqrt(HD))).astype(BF16)

    def head_mask(first, width, head):
        lane = iota((1, width), 1) + first
        return jnp.where(jnp.logical_and(lane >= head * HD, lane < (head + 1) * HD), 1.0, 0.0).astype(BF16)

    windows = []
    for p in range(HEADS // 2):
        first = (2 * p * HD) // 128 * 128
        last = -(-((2 * p + 2) * HD) // 128) * 128
        windows.append((first, last - first))
        block = kv[:, first:last]
        for e in range(2):
            km[p, e * TK:(e + 1) * TK, 0:last - first] = block * head_mask(first, last - first, 2 * p + e)
    value_heads = []
    for n in range(3):
        heads = [h for h in range(HEADS) if h * HD < (n + 1) * 256 and (h + 1) * HD > n * 256]
        value_heads.append(heads)
        block = kv[:, D + n * 256:D + (n + 1) * 256]
        for slot, h in enumerate(heads):
            vm[n, slot * TK:(slot + 1) * TK, :] = block * head_mask(n * 256, 256, h)

    def c_copy(owner):
        return remote(wmsg.at[rows_of(owner, OWN)], cbuf.at[c], csem, r, owner)

    c_all = remote(wmsg.at[other_rows], cbuf.at[others], csem, r, next_col)
    owners = CHUNK // OWN
    chunks = TQ // CHUNK

    def attend(step):
        chunk = jnp.bitwise_and(lax.shift_right_logical(c, 3) + step, chunks - 1)
        at = rows_of(chunk, CHUNK)
        mean = s1[at, :] * (1.0 / CA)
        mean_high, mean_low = split(mean)
        mean_high = mean_high.astype(F32)
        mean_low = mean - mean_high
        var = (s2[at, :] * (1.0 / CA) - mean_high * mean_high) - mean_low * (mean_high + mean)
        rstd = lax.rsqrt(jnp.maximum(var, 0.0) + 1e-05)
        lane = iota((CHUNK, 128), 1)
        tops = jnp.zeros((CHUNK, 128), F32)
        totals = jnp.zeros((CHUNK, 128), F32)
        for p in range(HEADS // 2):
            first, width = windows[p]
            scores = mm_nt(qv[at, first:first + width], km[p, :, 0:width])
            for e in range(2):
                h = 2 * p + e
                raw = bias[pl.ds(pl.multiple_of(h * TQ + chunk * CHUNK, CHUNK), CHUNK), :]
                sc = scores[:, e * TK:(e + 1) * TK] + (raw - mean * colsum[h:h + 1, :]) * rstd
                top = jnp.max(sc, axis=-1, keepdims=True)
                expo = jnp.exp(sc - top)
                total = jnp.sum(expo, axis=-1, keepdims=True)
                probs[:, h * TK:(h + 1) * TK] = expo.astype(BF16)
                tops = jnp.where(lane == h, top, tops)
                totals = jnp.where(lane == h, total, totals)
        for n in range(3):
            heads = value_heads[n]
            wide = probs[:, heads[0] * TK:(heads[-1] + 1) * TK]
            wmsg[at, n * 256:(n + 1) * 256] = mm(wide, vm[n]).astype(BF16)
        tops_high, tops_mid = split(tops)
        tops_low = (tops - tops_high.astype(F32) - tops_mid.astype(F32)).astype(BF16)
        totals_high, totals_low = split(totals)
        stats = tops_high.astype(F32)
        for place, piece in enumerate((tops_mid, tops_low, totals_high, totals_low)):
            stats = stats + pltpu.roll(piece.astype(F32), (place + 1) * HEADS, 1)
        wmsg[at, D:MSG] = stats.astype(BF16)

        return chunk

    def far_chunk(step, carry):
        chunk = attend(step)
        for k in range(owners):
            c_copy(chunk * owners + jnp.bitwise_and(c + turn * k, owners - 1)).start()
        return carry

    lax.fori_loop(1, chunks, far_chunk, 0)
    chunk = attend(0)
    for k in range(1, owners):
        c_copy(chunk * owners + jnp.bitwise_and(c + turn * k, owners - 1)).start()
    cbuf[c] = wmsg[own, :]
    mean_high, mean_low = split(mean_own[...])
    hidden_own = mm(mean_high, wagg[...]) + mm(mean_low, wagg[...]) + cond[own, :].astype(F32)
    spread_row = jnp.bitwise_and(iota((256, D), 0), 127)
    spread_col = iota((256, D), 1) - spread_row * HD
    expand[...] = jnp.where(jnp.logical_and(spread_col >= 0, spread_col < HD), 1.0, 0.0).astype(BF16)
    loads["wo"].wait()
    loads["wb"].wait()
    c_all.wait_recv()

    stat = cbuf[:, :, D:MSG].reshape(TQ, 128).astype(F32)
    def piece(k):
        return pltpu.roll(stat, 128 - k * HEADS, 1)

    tops = ((stat + piece(1)) + piece(2)).reshape(NCOL, OWN, 128)
    totals = (piece(3) + piece(4)).reshape(NCOL, OWN, 128)
    best = jnp.max(tops, axis=0, keepdims=True)
    scale = jnp.exp(tops - best)
    total = jnp.sum(scale * totals, axis=0, keepdims=True)
    valid = iota((1, 1, 128), 2) < HEADS
    total = jnp.where(valid, total, 1.0)
    factor = jnp.where(valid, scale / total, 0.0).reshape(TQ, 128)
    factor = jnp.concatenate(split(factor), axis=1)
    attn_parts = []
    for n in range(3):
        cols = slice(n * 256, (n + 1) * 256)
        wide = mm(factor, expand[:, cols])
        terms = cbuf[:, :, cols].astype(F32) * wide.reshape(NCOL, OWN, 256)
        attn_parts.append(jnp.sum(terms, axis=0).astype(BF16))
    attn = jnp.concatenate(attn_parts, axis=1)
    finished = (hidden_own + mm(attn, wo[...])).astype(BF16)

    tokbuf[c] = finished
    d_all = remote(tokbuf.at[others], tokbuf.at[others], dsem, r, next_col)
    def spread_to(peer):
        remote(tokbuf.at[c], tokbuf.at[c], dsem, r, peer).start()

    @pl.when(c != 0)
    def _():
        spread_to(0)

    for k in (8, 7, 6, 5, 4, 3, 2, 1, 15, 14, 13, 12, 11, 10, 9):
        @pl.when(col_at(turn * k) != 0)
        def _():
            spread_to(col_at(turn * k))


    a_all.wait_send()
    b_all.wait_send()

    @pl.when(holds)
    def _():
        for k in range(4):
            cond_copy(held_cond, sibling).wait_send()

    @pl.when(passes_on)
    def _():
        cond_copy(keycond, sibling).wait_send()

    from_sources(keymeans, ksem, lambda copy: copy.wait_send())
    c_all.wait_send()

    d_all.wait_recv()
    token_stores = quarters(tokbuf, token_out_h, osem)
    for copy in token_stores:
        copy.start()
    chosen = mm(pick[...], tokbuf[...].reshape(TQ, D)).astype(BF16)
    atomv[...] = (feats[...].astype(F32) + mm(chosen, wb[...])).astype(BF16)
    atom_store = pltpu.make_async_copy(atomv, atom_out_h, osem.at[4])
    atom_store.start()
    d_all.wait_send()
    for copy in token_stores:
        copy.wait()
    atom_store.wait()


def quarters(source, target, sems):
    parts = [pl.ds(k * (NCOL // 4), NCOL // 4) for k in range(4)]
    return [pltpu.make_async_copy(source.at[part], target.at[part], sems.at[k]) for k, part in enumerate(parts)]


def hand_over(token_in, atom_in, token_out, atom_out, sems):
    copies = quarters(token_in, token_out, sems) + [pltpu.make_async_copy(atom_in, atom_out, sems.at[4])]
    for copy in copies:
        copy.start()
    for copy in copies:
        copy.wait()


def local(
    atom_feats, atom_token, atom_counts, token_cond, pair, token_gain, pair_gain, w_bias, w_agg, w_query, w_keyval,
    w_out, w_back,
):
    any_space = pl.BlockSpec(memory_space=pl.ANY)
    hbm = pl.BlockSpec(memory_space=pltpu.HBM)
    vmem = pltpu.VMEM
    dma = pltpu.SemaphoreType.DMA
    scratch = [
        vmem((CA, CA), BF16), vmem((1, CA), jnp.int32), vmem((1, TQ), jnp.int32), vmem((TQ, D), BF16),
        vmem((TQ, TK, CA), BF16), vmem((6, 128), F32), vmem((1, CA), F32), vmem((HEADS, CA), BF16),
        vmem((CA, D), BF16), vmem((D, D), BF16), vmem((D, 2 * D), BF16), vmem((D, D), BF16), vmem((D, CA), BF16),
        vmem((3 * HEADS, 2 * CA), BF16), vmem((HEADS, CA), F32), vmem((HEADS * TQ, TK), F32), vmem((TQ, TK), F32),
        vmem((TQ, TK), F32), vmem((TQ, CA), BF16), vmem((NCOL, OWN, CA), BF16), vmem((TQ, CA), BF16), vmem((OWN, CA), F32),
        vmem((TQ, CA), F32),
        vmem((TQ, D), F32), vmem((TQ, D), BF16), vmem((TQ, D), BF16), vmem((TK, 2 * D), BF16),
        vmem((8, OWN, CA), BF16), vmem((TK, D), BF16),
        vmem((HEADS // 2, 2 * TK, 256), BF16), vmem((3, 6 * TK, 256), BF16), vmem((CHUNK, HEADS * TK), BF16),
        vmem((TQ, MSG), BF16), vmem((NCOL, OWN, MSG), BF16), vmem((256, D), BF16), vmem((NCOL, OWN, D), BF16),
        vmem((CA, TQ), BF16), vmem((CA, CA), BF16),
        dma((13,)), dma((PAIR_PARTS,)), dma((5,)),
        *[dma((2,))] * 6,
    ]
    outs = pl.pallas_call(
        kernel,
        out_shape=(jax.ShapeDtypeStruct((NCOL, OWN, D), BF16), jax.ShapeDtypeStruct((CA, CA), BF16)),
        in_specs=[hbm] * 13,
        out_specs=(any_space, any_space),
        scratch_shapes=scratch,
        compiler_params=pltpu.CompilerParams(
            collective_id=0, has_side_effects=True, vmem_limit_bytes=40 * 1024 * 1024),
        name="diffusion_block",
    )(*[pltpu.with_memory_space_constraint(x, pltpu.HBM) for x in (
        atom_feats, atom_token.reshape(1, CA), atom_counts.reshape(1, TQ), token_cond, pair, token_gain.reshape(6, 128),
        pair_gain.reshape(1, CA), w_bias.T, w_agg, w_query, w_keyval, w_out, w_back,
    )])
    stored = pl.pallas_call(
        hand_over,
        out_shape=(jax.ShapeDtypeStruct((NCOL, OWN, D), BF16), jax.ShapeDtypeStruct((CA, CA), BF16)),
        in_specs=[any_space] * 2,
        out_specs=(any_space, any_space),
        scratch_shapes=[dma((5,))],
        compiler_params=pltpu.CompilerParams(vmem_limit_bytes=1024 * 1024),
        name="hand_over",
    )(*outs)
    return stored[0].reshape(TQ, D), stored[1]


def solution(mesh):
    placed = (
        P(("row", "col"), None), P(("row", "col")), P("row"), P("row", None), P("row", "col", None),
        P(), P(), P(), P(), P(), P(), P(), P(),
    )
    return jax.shard_map(
        local,
        mesh=mesh,
        in_specs=placed,
        out_specs=(P("row", None), P(("row", "col"), None)),
        check_vma=False,
    )
```

```python
import math

import jax
import jax.numpy as jnp
from jax import lax
from jax.experimental import pallas as pl
from jax.experimental.pallas import tpu as pltpu
from jax.sharding import PartitionSpec as P

D = 768
HEADS = 16
HD = 48
CA = 128
TQ = 256
TK = 128
NCOL = 16
NROW = 8
OWN = TQ // NCOL
MSG = D + 128
CHUNK = 128
PAIR_PARTS = 8
PART_ROWS = TQ // PAIR_PARTS
FIRST_PARTS = 3
PASS_PART = 5
MESH = pl.DeviceIdType.MESH
F32 = jnp.float32
BF16 = jnp.bfloat16


def mm(a, b):
    return jnp.dot(a, b, preferred_element_type=F32)


def mm_nt(a, b):
    return lax.dot_general(a, b, (((1,), (1,)), ((), ())), preferred_element_type=F32)


def iota(shape, axis):
    return lax.broadcasted_iota(jnp.int32, shape, axis)


def split(x):
    high = x.astype(BF16)
    low = (x - high.astype(F32)).astype(BF16)
    return high, low


def rows_of(index, size):
    return pl.ds(pl.multiple_of(index * size, size), size)


def kernel(
    feats_h, tok_h, counts_h, cond_h, pair_h, tgain_h, pgain_h, wbias_h, wagg_h, wq_h, wkv_h, wo_h, wb_h,
    token_out_h, atom_out_h,
    feats, tok, counts, cond, pair, tgain, pgain, wbias, wagg, wq, wkv, wo, wb,
    gmat, colsum, bias, s1, s2, part, abuf, means, mean_own, cnt, aggv, normed, qv, kv, keymeans, keycond,
    km, vm, probs, wmsg, cbuf, expand, tokbuf, pick, atomv,
    lsem, psem, osem, asem, bsem, ksem, csem, qsem, dsem,
):
    r = lax.axis_index("row")
    c = lax.axis_index("col")
    key_col = 2 * r + lax.shift_right_logical(c, 3)
    key_slot = jnp.bitwise_and(c, 7)
    src_row = lax.shift_right_logical(c, 1)
    src_col = 8 * jnp.bitwise_and(c, 1)
    is_self = c == key_col
    other = jnp.logical_not(is_self)
    holds = r == src_row
    same_core = jnp.bitwise_and(r, 1) == jnp.bitwise_and(src_row, 1)
    sibling = jnp.bitwise_xor(r, 1)
    passes_on = jnp.logical_and(same_core, jnp.logical_not(holds))

    def col_at(offset):
        return jnp.bitwise_and(c + offset, NCOL - 1)

    next_col = col_at(1)
    turn = 1 - 2 * jnp.bitwise_and(r, 1)

    def local(i, src, dst):
        return pltpu.make_async_copy(src, dst, lsem.at[i])

    loads = {
        "feats": local(0, feats_h, feats),
        "tok": local(1, tok_h, tok),
        "counts": local(2, counts_h, counts),
        "wbias": local(3, wbias_h, wbias),
        "pgain": local(4, pgain_h, pgain),
        "wagg": local(5, wagg_h, wagg),
        "cond": local(7, cond_h, cond),
        "tgain": local(8, tgain_h, tgain),
        "wq": local(9, wq_h, wq),
        "wkv": local(10, wkv_h, wkv),
        "wo": local(11, wo_h, wo),
        "wb": local(12, wb_h, wb),
    }

    def pair_load(k):
        at = pl.ds(k * PART_ROWS, PART_ROWS)
        return pltpu.make_async_copy(pair_h.at[at], pair.at[at], psem.at[k])

    for name in ("feats", "tok", "counts", "wbias", "pgain"):
        loads[name].start()

    barrier = pltpu.get_barrier_semaphore()

    def greet(row, col):
        pl.semaphore_signal(barrier, inc=1, device_id=(row, col), device_id_type=MESH)

    for k in range(1, NCOL):
        greet(r, col_at(k))
    for k in range(1, 8):
        greet(src_row, src_col + jnp.bitwise_and(c + k, 7))

    @pl.when(other)
    def _():
        greet(src_row, src_col + key_slot)

    @pl.when(jnp.logical_not(holds))
    def _():
        greet(jnp.where(same_core, src_row, sibling), c)

    for k in range(3):
        pair_load(k).start()

    loads["feats"].wait()
    loads["tok"].wait()
    here = tok[...] - r * TQ
    member = jnp.where(iota((TQ, CA), 0) == here, 1.0, 0.0).astype(BF16)
    part[...] = mm(member, feats[...]).astype(BF16)

    pl.semaphore_wait(
        barrier,
        NCOL - 1 + 8 - is_self.astype(jnp.int32) + 4 * holds.astype(jnp.int32) + passes_on.astype(jnp.int32))

    def remote(src, dst, sems, row, col):
        return pltpu.make_async_remote_copy(
            src_ref=src, dst_ref=dst, send_sem=sems.at[0], recv_sem=sems.at[1],
            device_id=(row, col), device_id_type=MESH)

    others = pl.ds(0, NCOL - 1)
    other_rows = pl.ds(0, (NCOL - 1) * OWN)

    def a_copy(peer):
        return remote(part.at[rows_of(peer, OWN)], abuf.at[c], asem, r, peer)

    a_all = remote(part.at[other_rows], abuf.at[others], asem, r, next_col)

    def each_peer(action):
        for k in (8, 9, 10, 11, 12, 13, 14, 15, 1, 2, 3, 4, 5, 6, 7):
            action(col_at(turn * k))

    each_peer(lambda peer: a_copy(peer).start())
    for name in ("wagg", "cond", "tgain"):
        loads[name].start()
    for k in range(3, PAIR_PARTS):
        pair_load(k).start()
    for name in ("wq", "wkv", "wo", "wb"):
        loads[name].start()

    def each_target(action):
        for k in range(1, NROW):
            action(jnp.bitwise_and(r + k, NROW - 1))

        @pl.when(other)
        def _():
            action(r)

    def from_sources(buffer, sems, action):
        for count in (7, 8):
            @pl.when(is_self == (count == 7))
            def _():
                action(remote(buffer.at[pl.ds(0, count)], buffer.at[pl.ds(0, count)], sems, r, next_col))

    held_cond = cond_h.at[rows_of(jnp.bitwise_and(c, 1), TK)]

    def cond_copy(source, row):
        return remote(source, keycond, qsem, row, c)

    @pl.when(holds)
    def _():
        for k in (4, 2, 6):
            cond_copy(held_cond, jnp.bitwise_and(r + k, NROW - 1)).start()
        cond_copy(held_cond, sibling).start()

    abuf[c] = part[rows_of(c, OWN), :]

    eye = iota((CA, CA), 0) == iota((CA, CA), 1)
    eye_b = jnp.where(eye, 1.0, 0.0).astype(BF16)
    pick[...] = mm_nt(eye_b, member).astype(BF16)
    loads["wbias"].wait()
    loads["pgain"].wait()
    gain_t = (wbias[...].astype(F32) * pgain[...]).astype(BF16)
    none = jnp.zeros((HEADS, CA), BF16)
    place = iota((HEADS, CA), 0)
    ones_left = jnp.where(place == 0, 1.0, 0.0).astype(BF16)
    ones_right = jnp.where(place == 1, 1.0, 0.0).astype(BF16)
    gmat[:, 0:CA] = jnp.concatenate([gain_t, none, ones_left], axis=0)
    gmat[:, CA:2 * CA] = jnp.concatenate([none, gain_t, ones_right], axis=0)
    colsum[...] = jnp.broadcast_to(jnp.sum(gain_t.astype(F32), axis=1, keepdims=True), (HEADS, CA))
    loads["counts"].wait()
    for half in range(2):
        line = counts[:, half * CA:(half + 1) * CA].astype(F32)
        column = jnp.sum(jnp.where(eye, jnp.broadcast_to(line, (CA, CA)), 0.0), axis=1, keepdims=True)
        cnt[half * CA:(half + 1) * CA, :] = jnp.broadcast_to(column, (CA, CA))

    def bias_rows(k):
        pair_load(k).wait()

        def four(j, carry):
            first = k * PART_ROWS + 4 * j
            blocks = [jnp.transpose(pair[first + e]) for e in range(4)]
            for e in range(4):
                wide = blocks[e].astype(F32)
                s2[pl.ds(first + e, 1), :] = jnp.sum(wide * wide, axis=0, keepdims=True)
            square = jnp.concatenate(
                [jnp.concatenate(blocks[0:2], axis=1), jnp.concatenate(blocks[2:4], axis=1)], axis=0)
            sums = mm(gmat[...], square)
            for e in range(4):
                low, side = e // 2, slice((e % 2) * CA, (e % 2 + 1) * CA)
                bias[pl.ds(first + e, HEADS, stride=TQ), :] = sums[low * HEADS:(low + 1) * HEADS, side]
                s1[pl.ds(first + e, 1), :] = sums[2 * HEADS + low:2 * HEADS + low + 1, side]
            return carry

        lax.fori_loop(0, PART_ROWS // 4, four, 0, unroll=8)

    for k in range(FIRST_PARTS):
        bias_rows(k)

    a_all.wait_recv()
    own = rows_of(c, OWN)
    mean_own[...] = jnp.sum(abuf[...].astype(F32), axis=0) / cnt[own, :]
    means[own, :] = mean_own[...].astype(BF16)

    def k_copy(target):
        return remote(means.at[own], keymeans.at[key_slot], ksem, target, key_col)

    def b_copy(peer):
        return remote(means.at[own], means.at[own], bsem, r, peer)

    b_all = remote(means.at[other_rows], means.at[other_rows], bsem, r, next_col)
    each_target(lambda target: k_copy(target).start())
    each_peer(lambda peer: b_copy(peer).start())

    @pl.when(is_self)
    def _():
        keymeans[key_slot] = means[own, :]

    for k in range(FIRST_PARTS, PASS_PART):
        bias_rows(k)

    @pl.when(passes_on)
    def _():
        arrived = cond_copy(keycond, sibling)
        arrived.wait_recv()
        arrived.start()

    for k in range(PASS_PART, PAIR_PARTS):
        bias_rows(k)

    def normalize(hidden):
        center = hidden - jnp.mean(hidden, axis=-1, keepdims=True)
        spread = jnp.mean(center * center, axis=-1, keepdims=True)
        gain = jnp.concatenate([tgain[k:k + 1, :] for k in range(6)], axis=1)
        return (center * lax.rsqrt(spread + 1e-05) * gain).astype(BF16)

    for name in ("wagg", "cond", "tgain", "wq", "wkv"):
        loads[name].wait()
    @pl.when(holds)
    def _():
        keycond[...] = cond[rows_of(jnp.bitwise_and(c, 1), TK), :]

    @pl.when(jnp.logical_not(same_core))
    def _():
        cond_copy(keycond, sibling).wait_recv()

    from_sources(keymeans, ksem, lambda copy: copy.wait_recv())
    b_all.wait_recv()
    key_agg = mm(keymeans[...].reshape(TK, CA), wagg[...])
    aggv[...] = mm(means[...], wagg[...])
    key_rows = normalize(key_agg + keycond[...].astype(F32))
    for n in range(6):
        cols = slice(n * 256, (n + 1) * 256)
        kv[:, cols] = mm(key_rows, wkv[:, cols]).astype(BF16)
    for k in range(TQ // 64):
        at = slice(k * 64, (k + 1) * 64)
        normed[at, :] = normalize(aggv[at, :] + cond[at, :].astype(F32))
    for n in range(3):
        cols = slice(n * 256, (n + 1) * 256)
        qv[:, cols] = (mm(normed[...], wq[:, cols]) * (1.0 / math.sqrt(HD))).astype(BF16)

    def head_mask(first, width, head):
        lane = iota((1, width), 1) + first
        return jnp.where(jnp.logical_and(lane >= head * HD, lane < (head + 1) * HD), 1.0, 0.0).astype(BF16)

    windows = []
    for p in range(HEADS // 2):
        first = (2 * p * HD) // 128 * 128
        last = -(-((2 * p + 2) * HD) // 128) * 128
        windows.append((first, last - first))
        block = kv[:, first:last]
        for e in range(2):
            km[p, e * TK:(e + 1) * TK, 0:last - first] = block * head_mask(first, last - first, 2 * p + e)
    value_heads = []
    for n in range(3):
        heads = [h for h in range(HEADS) if h * HD < (n + 1) * 256 and (h + 1) * HD > n * 256]
        value_heads.append(heads)
        block = kv[:, D + n * 256:D + (n + 1) * 256]
        for slot, h in enumerate(heads):
            vm[n, slot * TK:(slot + 1) * TK, :] = block * head_mask(n * 256, 256, h)

    def c_copy(owner):
        return remote(wmsg.at[rows_of(owner, OWN)], cbuf.at[c], csem, r, owner)

    c_all = remote(wmsg.at[other_rows], cbuf.at[others], csem, r, next_col)
    owners = CHUNK // OWN
    chunks = TQ // CHUNK

    def attend(step):
        chunk = jnp.bitwise_and(lax.shift_right_logical(c, 3) + step, chunks - 1)
        at = rows_of(chunk, CHUNK)
        mean = s1[at, :] * (1.0 / CA)
        mean_high, mean_low = split(mean)
        mean_high = mean_high.astype(F32)
        mean_low = mean - mean_high
        var = (s2[at, :] * (1.0 / CA) - mean_high * mean_high) - mean_low * (mean_high + mean)
        rstd = lax.rsqrt(jnp.maximum(var, 0.0) + 1e-05)
        lane = iota((CHUNK, 128), 1)
        tops = jnp.zeros((CHUNK, 128), F32)
        totals = jnp.zeros((CHUNK, 128), F32)
        for p in range(HEADS // 2):
            first, width = windows[p]
            scores = mm_nt(qv[at, first:first + width], km[p, :, 0:width])
            for e in range(2):
                h = 2 * p + e
                raw = bias[pl.ds(pl.multiple_of(h * TQ + chunk * CHUNK, CHUNK), CHUNK), :]
                sc = scores[:, e * TK:(e + 1) * TK] + (raw - mean * colsum[h:h + 1, :]) * rstd
                top = jnp.max(sc, axis=-1, keepdims=True)
                expo = jnp.exp(sc - top)
                total = jnp.sum(expo, axis=-1, keepdims=True)
                probs[:, h * TK:(h + 1) * TK] = expo.astype(BF16)
                tops = jnp.where(lane == h, top, tops)
                totals = jnp.where(lane == h, total, totals)
        for n in range(3):
            heads = value_heads[n]
            wide = probs[:, heads[0] * TK:(heads[-1] + 1) * TK]
            wmsg[at, n * 256:(n + 1) * 256] = mm(wide, vm[n]).astype(BF16)
        tops_high, tops_mid = split(tops)
        tops_low = (tops - tops_high.astype(F32) - tops_mid.astype(F32)).astype(BF16)
        totals_high, totals_low = split(totals)
        stats = tops_high.astype(F32)
        for place, piece in enumerate((tops_mid, tops_low, totals_high, totals_low)):
            stats = stats + pltpu.roll(piece.astype(F32), (place + 1) * HEADS, 1)
        wmsg[at, D:MSG] = stats.astype(BF16)

        return chunk

    def far_chunk(step, carry):
        chunk = attend(step)
        for k in range(owners):
            c_copy(chunk * owners + jnp.bitwise_and(c + turn * k, owners - 1)).start()
        return carry

    lax.fori_loop(1, chunks, far_chunk, 0)
    chunk = attend(0)
    for k in range(1, owners):
        c_copy(chunk * owners + jnp.bitwise_and(c + turn * k, owners - 1)).start()
    cbuf[c] = wmsg[own, :]
    mean_high, mean_low = split(mean_own[...])
    hidden_own = mm(mean_high, wagg[...]) + mm(mean_low, wagg[...]) + cond[own, :].astype(F32)
    spread_row = jnp.bitwise_and(iota((256, D), 0), 127)
    spread_col = iota((256, D), 1) - spread_row * HD
    expand[...] = jnp.where(jnp.logical_and(spread_col >= 0, spread_col < HD), 1.0, 0.0).astype(BF16)
    loads["wo"].wait()
    loads["wb"].wait()
    c_all.wait_recv()

    stat = cbuf[:, :, D:MSG].reshape(TQ, 128).astype(F32)
    def piece(k):
        return pltpu.roll(stat, 128 - k * HEADS, 1)

    tops = ((stat + piece(1)) + piece(2)).reshape(NCOL, OWN, 128)
    totals = (piece(3) + piece(4)).reshape(NCOL, OWN, 128)
    best = jnp.max(tops, axis=0, keepdims=True)
    scale = jnp.exp(tops - best)
    total = jnp.sum(scale * totals, axis=0, keepdims=True)
    valid = iota((1, 1, 128), 2) < HEADS
    total = jnp.where(valid, total, 1.0)
    factor = jnp.where(valid, scale / total, 0.0).reshape(TQ, 128)
    factor = jnp.concatenate(split(factor), axis=1)
    attn_parts = []
    for n in range(3):
        cols = slice(n * 256, (n + 1) * 256)
        wide = mm(factor, expand[:, cols])
        terms = cbuf[:, :, cols].astype(F32) * wide.reshape(NCOL, OWN, 256)
        attn_parts.append(jnp.sum(terms, axis=0).astype(BF16))
    attn = jnp.concatenate(attn_parts, axis=1)
    finished = (hidden_own + mm(attn, wo[...])).astype(BF16)

    tokbuf[c] = finished
    d_all = remote(tokbuf.at[others], tokbuf.at[others], dsem, r, next_col)
    def spread_to(peer):
        remote(tokbuf.at[c], tokbuf.at[c], dsem, r, peer).start()

    @pl.when(c != 0)
    def _():
        spread_to(0)

    for k in (8, 7, 6, 5, 4, 3, 2, 1, 15, 14, 13, 12, 11, 10, 9):
        @pl.when(col_at(turn * k) != 0)
        def _():
            spread_to(col_at(turn * k))


    a_all.wait_send()
    b_all.wait_send()

    @pl.when(holds)
    def _():
        for k in range(4):
            cond_copy(held_cond, sibling).wait_send()

    @pl.when(passes_on)
    def _():
        cond_copy(keycond, sibling).wait_send()

    from_sources(keymeans, ksem, lambda copy: copy.wait_send())
    c_all.wait_send()

    d_all.wait_recv()
    token_store = pltpu.make_async_copy(tokbuf, token_out_h, osem.at[0])
    token_store.start()
    chosen = mm(pick[...], tokbuf[...].reshape(TQ, D)).astype(BF16)
    atomv[...] = (feats[...].astype(F32) + mm(chosen, wb[...])).astype(BF16)
    atom_store = pltpu.make_async_copy(atomv, atom_out_h, osem.at[1])
    atom_store.start()
    d_all.wait_send()
    token_store.wait()
    atom_store.wait()


def hand_over(token_in, atom_in, token_out, atom_out, sems):
    copies = [
        pltpu.make_async_copy(token_in, token_out, sems.at[0]),
        pltpu.make_async_copy(atom_in, atom_out, sems.at[1]),
    ]
    for copy in copies:
        copy.start()
    for copy in copies:
        copy.wait()


def local(
    atom_feats, atom_token, atom_counts, token_cond, pair, token_gain, pair_gain, w_bias, w_agg, w_query, w_keyval,
    w_out, w_back,
):
    any_space = pl.BlockSpec(memory_space=pl.ANY)
    hbm = pl.BlockSpec(memory_space=pltpu.HBM)
    vmem = pltpu.VMEM
    dma = pltpu.SemaphoreType.DMA
    scratch = [
        vmem((CA, CA), BF16), vmem((1, CA), jnp.int32), vmem((1, TQ), jnp.int32), vmem((TQ, D), BF16),
        vmem((TQ, TK, CA), BF16), vmem((6, 128), F32), vmem((1, CA), F32), vmem((HEADS, CA), BF16),
        vmem((CA, D), BF16), vmem((D, D), BF16), vmem((D, 2 * D), BF16), vmem((D, D), BF16), vmem((D, CA), BF16),
        vmem((3 * HEADS, 2 * CA), BF16), vmem((HEADS, CA), F32), vmem((HEADS * TQ, TK), F32), vmem((TQ, TK), F32),
        vmem((TQ, TK), F32), vmem((TQ, CA), BF16), vmem((NCOL, OWN, CA), BF16), vmem((TQ, CA), BF16), vmem((OWN, CA), F32),
        vmem((TQ, CA), F32),
        vmem((TQ, D), F32), vmem((TQ, D), BF16), vmem((TQ, D), BF16), vmem((TK, 2 * D), BF16),
        vmem((8, OWN, CA), BF16), vmem((TK, D), BF16),
        vmem((HEADS // 2, 2 * TK, 256), BF16), vmem((3, 6 * TK, 256), BF16), vmem((CHUNK, HEADS * TK), BF16),
        vmem((TQ, MSG), BF16), vmem((NCOL, OWN, MSG), BF16), vmem((256, D), BF16), vmem((NCOL, OWN, D), BF16),
        vmem((CA, TQ), BF16), vmem((CA, CA), BF16),
        dma((13,)), dma((PAIR_PARTS,)), dma((2,)),
        *[dma((2,))] * 6,
    ]
    outs = pl.pallas_call(
        kernel,
        out_shape=(jax.ShapeDtypeStruct((NCOL, OWN, D), BF16), jax.ShapeDtypeStruct((CA, CA), BF16)),
        in_specs=[hbm] * 13,
        out_specs=(any_space, any_space),
        scratch_shapes=scratch,
        compiler_params=pltpu.CompilerParams(
            collective_id=0, has_side_effects=True, vmem_limit_bytes=40 * 1024 * 1024),
        name="diffusion_block",
    )(*[pltpu.with_memory_space_constraint(x, pltpu.HBM) for x in (
        atom_feats, atom_token.reshape(1, CA), atom_counts.reshape(1, TQ), token_cond, pair, token_gain.reshape(6, 128),
        pair_gain.reshape(1, CA), w_bias.T, w_agg, w_query, w_keyval, w_out, w_back,
    )])
    stored = pl.pallas_call(
        hand_over,
        out_shape=(jax.ShapeDtypeStruct((NCOL, OWN, D), BF16), jax.ShapeDtypeStruct((CA, CA), BF16)),
        in_specs=[any_space] * 2,
        out_specs=(any_space, any_space),
        scratch_shapes=[dma((2,))],
        compiler_params=pltpu.CompilerParams(vmem_limit_bytes=1024 * 1024),
        name="hand_over",
    )(*outs)
    return stored[0].reshape(TQ, D), stored[1]


def solution(mesh):
    placed = (
        P(("row", "col"), None), P(("row", "col")), P("row"), P("row", None), P("row", "col", None),
        P(), P(), P(), P(), P(), P(), P(), P(),
    )
    return jax.shard_map(
        local,
        mesh=mesh,
        in_specs=placed,
        out_specs=(P("row", None), P(("row", "col"), None)),
        check_vma=False,
    )
```
